512 devices in a mesh: gz: 128 (over y, z, core), gy: 4 (over x).
Axes of the slice: x: 4, y: 8, z: 8, core: 2. Of those that a mesh axis runs over, the one named last changes fastest.
Arguments:
- image: bfloat16 [128, 512, 512], P('gz', 'gy'), may hold values from -30 to 30, as said below
- conv_one: bfloat16 [16, 9], replicated, may hold values from -2 to 2
- conv_two: bfloat16 [32, 144], replicated, may hold values from -0.5 to 0.5
- tissue: int32 [128, 4096], P('gz', 'gy'), may hold values 0 or 1
Outputs:
- increments: float32 [2, 128, 4096], P(None, 'gz', 'gy')
The draws below stay inside these ranges and needn't reach their ends.
Inputs may be any that keep to these rules, and one draw needn't show every extreme that they name: `image`: pixel intensities of each section's crop.
All inputs are finite; a program needn't handle non-finite values. No bound on the sum of `tissue` on one device may be relied on, other than what follows from the above.
Results may differ from the reference program's by a relative error of at most 0.0029.
Values may be sent and summed in bfloat16 or wider, within the bound.
A program may use at most 64 MiB of HBM per device.

```python
import jax
import jax.numpy as jnp
from jax import lax

CROP = 512
NODES = 64
CH_ONE = 16
CH_TWO = 32
REACH = 6
SECTIONS = 128


def draw_image(key, part):
    shape = (SECTIONS, CROP, CROP)
    result = jnp.clip(jax.random.normal(key, shape, jnp.float32), -6.0, 6.0)
    return result.astype(jnp.bfloat16)


def with_ends(values, rng, least, largest):
    dims = values.shape
    place = [jax.random.randint(jax.random.fold_in(rng, axis), (), 0, dims[axis]) for axis in range(len(dims))]
    values = values.at[tuple(place)].set(least)
    longest = dims.index(max(dims))
    place[longest] = (place[longest] + 1) % dims[longest]
    return values.at[tuple(place)].set(largest)


def bell_draw(rng, shape, width, bound, kind=jnp.bfloat16):
    values = width * jax.random.normal(rng, shape, jnp.float32)
    return jnp.clip(values, min=-bound, max=bound).astype(kind)


def setup_inputs(seed: int = 0) -> dict:
    streams_of = jax.random.split(jax.random.key(seed), 5)
    image = draw_image(jax.random.fold_in(streams_of[4], 71), 0)
    conv_one = bell_draw(streams_of[1], (CH_ONE, 9), 9 ** -0.5, 2.0)
    conv_two = bell_draw(streams_of[2], (CH_TWO, 9 * CH_ONE), (9 * CH_ONE) ** -0.5, 0.5)
    tissue = with_ends((jax.random.randint(streams_of[3], (SECTIONS, NODES * NODES), 0, 4) < 3).astype(jnp.int32), jax.random.fold_in(streams_of[3], 1), 0, 1)
    return {"image": image, "conv_one": conv_one, "conv_two": conv_two, "tissue": tissue}


spring_rate = 8.0
anchor_rate = 0.02
prior_var = 1.0


def first_conv(pixels, weights):
    height = (pixels.shape[0] - 1) // 2
    extent = pixels.shape[1]
    padded = jnp.pad(pixels, ((0, 0), (1, 0)))
    stencil = jnp.stack([padded[offset_row:offset_row + 2 * height:2, offset_col:offset_col + extent:2] for offset_row in range(3) for offset_col in range(3)])
    summed = jnp.dot(weights, stencil.reshape(9, -1), preferred_element_type=jnp.float32)
    return jnp.maximum(summed, 0.0).astype(jnp.bfloat16).reshape(weights.shape[0], height, extent // 2)


def second_conv(layers, weights):
    height = (layers.shape[1] - 1) // 2
    extent = layers.shape[2]
    padded = jnp.pad(layers, ((0, 0), (0, 0), (1, 0)))
    stencil = jnp.stack([padded[:, offset_row:offset_row + 2 * height:2, offset_col:offset_col + extent:2] for offset_row in range(3) for offset_col in range(3)], axis=1)
    summed = jnp.dot(weights, stencil.reshape(weights.shape[1], -1), preferred_element_type=jnp.float32)
    return jnp.maximum(summed, 0.0).astype(jnp.bfloat16).reshape(weights.shape[0], height, extent // 2)


def correlate(own, window, patch):
    channels, total_rows, extent = own.shape
    reach = (window.shape[1] - total_rows) // 2
    block = min(32, total_rows)
    span = 2 * reach + 1
    offsets = lax.broadcasted_iota(jnp.int32, (span * span, 1, 1), 0)
    shift_row = (offsets // span - reach).astype(jnp.float32)
    shift_col = (offsets % span - reach).astype(jnp.float32)

    def one_block(number):
        start = number * block
        mine = lax.dynamic_slice_in_dim(own, start, block, 1).astype(jnp.float32)
        theirs = lax.dynamic_slice_in_dim(window, start, block + 2 * reach, 1).astype(jnp.float32)
        scores = jnp.stack([jnp.sum(mine * theirs[:, offset_row:offset_row + block, offset_col:offset_col + extent], axis=0) for offset_row in range(span) for offset_col in range(span)]) * channels ** -0.5
        highest = jnp.max(scores, axis=0, keepdims=True)
        expo = jnp.exp(scores - highest)
        prob = expo / jnp.sum(expo, axis=0, keepdims=True)
        mean_row = jnp.sum(prob * shift_row, axis=0)
        mean_col = jnp.sum(prob * shift_col, axis=0)
        var_row = jnp.sum(prob * shift_row * shift_row, axis=0) - mean_row * mean_row + prior_var
        var_col = jnp.sum(prob * shift_col * shift_col, axis=0) - mean_col * mean_col + prior_var
        covar = jnp.sum(prob * shift_row * shift_col, axis=0) - mean_row * mean_col
        determ = var_row * var_col - covar * covar
        info_rr = var_col / determ
        info_rc = -covar / determ
        info_cc = var_row / determ
        pull_row = info_rr * mean_row + info_rc * mean_col
        pull_col = info_rc * mean_row + info_cc * mean_col
        fields = jnp.stack([info_rr, info_rc, info_cc, pull_row, pull_col])
        return fields.reshape(5, block // patch, patch, extent // patch, patch).mean(axis=(2, 4))

    pooled = lax.map(one_block, jnp.arange(total_rows // block, dtype=jnp.int32))
    return jnp.transpose(pooled, (1, 0, 2, 3)).reshape(5, -1)


def times_two(left, right):
    return (left[0] * right[0] + left[1] * right[2], left[0] * right[1] + left[1] * right[3], left[2] * right[0] + left[3] * right[2], left[2] * right[1] + left[3] * right[3])


def invert_two(matrix):
    determ = matrix[0] * matrix[3] - matrix[1] * matrix[2]
    return (matrix[3] / determ, -matrix[1] / determ, -matrix[2] / determ, matrix[0] / determ)


def apply_two(matrix, vector):
    return (matrix[0] * vector[0] + matrix[1] * vector[1], matrix[2] * vector[0] + matrix[3] * vector[1])


def minus_parts(left, right):
    return tuple(first - second for first, second in zip(left, right))


def negate_parts(parts):
    return tuple(-member for member in parts)


def lower_parts(parts):
    return tuple(jnp.concatenate([jnp.zeros_like(member[:1]), member[:-1]], axis=0) for member in parts)


def upper_parts(parts):
    return tuple(jnp.concatenate([member[1:], jnp.zeros_like(member[:1])], axis=0) for member in parts)


def pick_parts(parts, first):
    return tuple(member[first::2] for member in parts)


def reduce_solve(diag, below, above, rhs):
    count = diag[0].shape[0]
    if count == 1:
        return apply_two(invert_two(diag), rhs)
    inv_odd = invert_two(pick_parts(diag, 1))
    below_odd = pick_parts(below, 1)
    above_odd = pick_parts(above, 1)
    rhs_odd = pick_parts(rhs, 1)
    alpha = times_two(pick_parts(below, 0), lower_parts(inv_odd))
    gamma = times_two(pick_parts(above, 0), inv_odd)
    new_diag = minus_parts(minus_parts(pick_parts(diag, 0), times_two(alpha, lower_parts(above_odd))), times_two(gamma, below_odd))
    new_below = negate_parts(times_two(alpha, lower_parts(below_odd)))
    new_above = negate_parts(times_two(gamma, above_odd))
    new_rhs = minus_parts(minus_parts(pick_parts(rhs, 0), apply_two(alpha, lower_parts(rhs_odd))), apply_two(gamma, rhs_odd))
    solved_even = reduce_solve(new_diag, new_below, new_above, new_rhs)
    residue = minus_parts(minus_parts(rhs_odd, apply_two(below_odd, solved_even)), apply_two(above_odd, upper_parts(solved_even)))
    solved_odd = apply_two(inv_odd, residue)
    return tuple(jnp.stack([even, odd], axis=1).reshape((count,) + even.shape[1:]) for even, odd in zip(solved_even, solved_odd))


def pad_to(member, total, value):
    extra = total - member.shape[0]
    if extra == 0:
        return member
    return jnp.concatenate([member, jnp.full((extra,) + member.shape[1:], value, member.dtype)], axis=0)


def solve_columns(blocks):
    count = blocks[0].shape[0]
    index = lax.broadcasted_iota(jnp.int32, blocks[0].shape, 0)
    neighbours = (index > 0).astype(jnp.float32) + (index < count - 1).astype(jnp.float32)
    extra = spring_rate * neighbours + anchor_rate
    zeros = jnp.zeros_like(blocks[0])
    coupling_low = jnp.where(index > 0, -spring_rate, zeros)
    coupling_high = jnp.where(index < count - 1, -spring_rate, zeros)
    total = 1 << (count - 1).bit_length()
    diag = (pad_to(blocks[0] + extra, total, 1.0), pad_to(blocks[1], total, 0.0), pad_to(blocks[1], total, 0.0), pad_to(blocks[2] + extra, total, 1.0))
    below = tuple(pad_to(member, total, 0.0) for member in (coupling_low, zeros, zeros, coupling_low))
    above = tuple(pad_to(member, total, 0.0) for member in (coupling_high, zeros, zeros, coupling_high))
    rhs = (pad_to(blocks[3], total, 0.0), pad_to(blocks[4], total, 0.0))
    solved = reduce_solve(diag, below, above, rhs)
    return tuple(member[:count] for member in solved)


def section_features(pixels, conv_one, conv_two):
    first = first_conv(jnp.concatenate([jnp.zeros((1, pixels.shape[1]), jnp.bfloat16), pixels], axis=0), conv_one)
    top = jnp.zeros((first.shape[0], 1, first.shape[2]), jnp.bfloat16)
    return second_conv(jnp.concatenate([top, first], axis=1), conv_two)


def reference(image, conv_one, conv_two, tissue):
    patch = CROP // (4 * NODES)

    def step(following, inputs):
        pixels, marks, position = inputs
        own = section_features(pixels, conv_one, conv_two)
        window = jnp.pad(following, ((0, 0), (REACH, REACH), (REACH, REACH)))
        data = correlate(own, window, patch)
        keep = marks.astype(jnp.float32) * (position < SECTIONS - 1).astype(jnp.float32)
        return own, data * keep[None, :]

    start = jnp.zeros((CH_TWO, CROP // 4, CROP // 4), jnp.bfloat16)
    positions = jnp.arange(SECTIONS, dtype=jnp.int32)
    unused, data = lax.scan(step, start, (image, tissue, positions), reverse=True)
    blocks = tuple(data[:, number, :] for number in range(5))
    return jnp.stack(solve_columns(blocks))
```

```python
import jax
import jax.numpy as jnp
from jax import lax
from jax.experimental import pallas as pl
from jax.experimental.pallas import tpu as pltpu
from jax.sharding import PartitionSpec as P

BF, F32 = jnp.bfloat16, jnp.float32
MESH = pl.DeviceIdType.MESH
GROUP = 16
SPRING, ANCHOR = 8.0, 0.02
ROWS = 32
SCALE = 32 ** (-0.5) * 1.4426950408889634


def iota(shape, dim):
    return lax.broadcasted_iota(jnp.int32, shape, dim)


def mm(left, right):
    return jnp.dot(left, right, preferred_element_type=F32)


def half_turn(x):
    return pltpu.roll(x, 64, 1)


def inv_sym(a, b, c):
    r = 1.0 / (a * c - b * b)
    return c * r, -b * r, a * r


def mul22(l, r):
    return (
        l[0] * r[0] + l[1] * r[2],
        l[0] * r[1] + l[1] * r[3],
        l[2] * r[0] + l[3] * r[2],
        l[2] * r[1] + l[3] * r[3],
    )


def mul21(l, v):
    return l[0] * v[0] + l[1] * v[1], l[2] * v[0] + l[3] * v[1]


def full(sym):
    return sym[0], sym[1], sym[1], sym[2]


def build_weights(w1_ref, w2_ref, sel, w1b, w2p):
    for part in range(4):
        base = iota((128, 128), 0) + 128 * part - 4 * iota((128, 128), 1)
        for v in range(7):
            sel[128 * part : 128 * part + 128, 128 * v : 128 * v + 128] = jnp.where(
                base == v - 3, 1.0, 0.0
            ).astype(BF)
    tap, col = iota((9, 256), 0), iota((9, 256), 1)
    a = (tap * 11) >> 5
    da = (col & 31) - 15 - a
    db = (col >> 5) - (tap - 3 * a)
    w1 = w1_ref[...]
    base = jnp.concatenate(
        [mm(w1, jnp.where((da == 0) & (db == 2 * b), 1.0, 0.0).astype(BF)) for b in range(3)], axis=0
    )
    for f in range(8):
        moved = base if f == 0 else pltpu.roll(base, 2 * f, 1)
        w1b[48 * f : 48 * f + 48, :] = moved[:, :224].astype(BF)
    k, n = iota((144, 144), 0), iota((144, 144), 1)
    ab = n >> 4
    perm = jnp.where(k == 9 * (n & 15) + ab, 1.0, 0.0).astype(BF)
    w2p[...] = mm(w2_ref[...], perm).astype(BF)


def split_columns(window, rows, sel, xs):
    for pair in range(4):
        width = 256 if pair < 3 else 128
        out = mm(window[...], sel[:, 256 * pair : 256 * pair + width]).astype(BF)
        xs[2 * pair, 16 : 16 + rows, :] = out[:, :128]
        if pair < 3:
            xs[2 * pair + 1, 16 : 16 + rows, :] = out[:, 128:]


def conv_rows(xs, w1b, fm, half, low):
    def column(block):
        start = pl.multiple_of(16 * block, 16)
        return jnp.concatenate([xs[v, pl.ds(start, 32), :] for v in range(7)], axis=0)

    right = jnp.concatenate([column(low), column(low + half)], axis=1)
    out = jnp.maximum(mm(w1b[...], right), 0.0).astype(BF)
    fm[pl.ds(pl.multiple_of(384 * low, 128), 384), :] = out[:, :128]
    fm[pl.ds(pl.multiple_of(384 * (low + half), 128), 384), :] = out[:, 128:]


def conv_features(fm, w2p, first, count):
    right = jnp.concatenate(
        [fm[pl.ds(pl.multiple_of(96 * (first + q) - 48, 16), 144), :] for q in range(count)], axis=1
    )
    return jnp.maximum(mm(w2p[...], right), 0.0).astype(BF).astype(F32)


def own_pair(fm, w2p, rall, p):
    feats = conv_features(fm, w2p, 4 + 2 * p, 2)
    chunk = (iota((32, 256), 1) & 127) >> 4
    rall[p] = jnp.concatenate(
        [jnp.where(chunk == m, feats, 0.0) for m in range(8)], axis=0
    ).astype(BF)


def next_group(fm, w2p, lall, row_base, g):
    feats = conv_features(fm, w2p, 4 * g + 2, 4)
    stack = jnp.concatenate(
        [
            feats[:, 128 * q : 128 * q + 128] * (row_base + 4 * g + q < 128).astype(F32)
            for q in range(4)
        ],
        axis=0,
    )
    turned = pltpu.roll(stack, 6, 1).T
    inside = iota((128, 128), 0) >= 6
    body = jnp.where(inside, turned, 0.0)
    tail = jnp.where(inside[:16], 0.0, turned[:16])
    ext = jnp.concatenate([body, tail], axis=0)
    rot = [ext] + [pltpu.roll(ext, 32 * k, 1) for k in range(1, 4)]
    lane = iota((32, 128), 1) >> 5
    for q in range(4):
        halves = []
        for h in range(2):
            pick = [rot[(g4 - q) % 4][64 * h + 16 * g4 : 64 * h + 16 * g4 + 32] for g4 in range(4)]
            halves.append(
                jnp.where(
                    lane < 2,
                    jnp.where(lane == 0, pick[0], pick[1]),
                    jnp.where(lane == 2, pick[2], pick[3]),
                )
            )
        lall[pl.ds(pl.multiple_of(128 * g + 32 * q, 32), 32), :] = jnp.concatenate(
            halves, axis=1
        ).astype(BF)


def correlate_pair(lall, rall, scores, mom, p):
    scores[...] = mm(lall[pl.ds(pl.multiple_of(64 * p, 64), 14 * ROWS), :], rall[p])
    shift = iota((ROWS, 128), 0) - (iota((ROWS, 128), 1) & 15)
    valid = (shift >= 0) & (shift <= 12)
    b = (shift - 6).astype(F32)
    for par in range(2):
        cols = slice(128 * par, 128 * par + 128)

        def at(n):
            return scores[ROWS * (n + par) : ROWS * (n + par) + ROWS, cols]

        high = at(0)
        for n in range(1, 13):
            high = jnp.maximum(high, at(n))
        top = jnp.max(jnp.where(valid, high, -3e38), axis=0, keepdims=True)
        t0 = t1 = t2 = None
        for n in range(12, -1, -1):
            e = jnp.exp2((at(n) - top) * SCALE)
            t0 = e if t0 is None else t0 + e
            t1 = t0 if t1 is None else t1 + t0
            t2 = t1 if t2 is None else t2 + t1
        t0 = jnp.where(valid, t0, 0.0)
        t1 = jnp.where(valid, t1, 0.0)
        t2 = jnp.where(valid, t2, 0.0)
        tb = t0 * b
        for field, term in enumerate((t0, t1, t2, tb, tb * b, t1 * b)):
            mom[p, field : field + 1, cols] = jnp.sum(term, axis=0, keepdims=True)


def node_blocks(mom, marks_ref, last, send):
    m0, m1, m2, mb, mbb, mab = (mom[:, f, :] for f in range(6))
    r = 1.0 / m0
    n1, mean_b = m1 * r, mb * r
    mean_a = n1 - 7.0
    var_a = (2.0 * m2 - 15.0 * m1) * r + 49.0 - mean_a * mean_a + 1.0
    var_b = mbb * r - mean_b * mean_b + 1.0
    cov = mab * r - n1 * mean_b
    i_aa, i_ab, i_bb = inv_sym(var_a, cov, var_b)
    p_a = i_aa * mean_a + i_ab * mean_b
    p_b = i_ab * mean_a + i_bb * mean_b
    stack = jnp.concatenate([x[:, :128] + x[:, 128:] for x in (i_aa, i_ab, i_bb, p_a, p_b)], axis=0)
    pool = jnp.where((iota((128, 128), 0) >> 1) == (iota((128, 128), 1) & 63), 0.25, 0.0)
    pooled = jnp.dot(stack, pool, precision=lax.Precision.HIGHEST, preferred_element_type=F32)
    spread = jnp.where((iota((16, 8), 0) >> 1) == iota((16, 8), 1), 1.0, 0.0)
    marks = mm(spread, marks_ref[...].astype(F32))
    same = (iota((16, 128), 0) & 1) == (iota((16, 128), 1) >> 6)
    marks = jnp.where(same, marks, half_turn(marks)) * jnp.where(last, 0.0, 1.0)
    for f in range(5):
        data = pooled[16 * f : 16 * f + 16] * marks
        for q in range(16):
            send[q, f : f + 1, :] = data[q : q + 1]


def segment(recv, group, sections, low, high):
    left = iota((1, 128), 1) < 64
    first = None
    for j in range(GROUP):
        a, b, c, ra, rb = (
            jnp.where(left, recv[j, f : f + 1, :], recv[GROUP - 1 - j, f : f + 1, :]) for f in range(5)
        )
        section = GROUP * group + jnp.where(left, j, GROUP - 1 - j)
        ends = (section == 0) | (section == sections - 1)
        extra = jnp.where(ends, SPRING + ANCHOR, 2 * SPRING + ANCHOR)
        a, c = a + extra, c + extra
        if j == 0:
            d, y = (a, b, c), (ra, rb)
            eight, none = jnp.full((1, 128), SPRING), jnp.zeros((1, 128))
            cc = (eight, none, none, eight)
        else:
            inv = tuple(SPRING * x for x in inv_sym(*d))
            iy = mul21(full(inv), y)
            d = (a - SPRING * inv[0], b - SPRING * inv[1], c - SPRING * inv[2])
            y = (ra + iy[0], rb + iy[1])
            cc = mul22(full(inv), cc)
        rows = d + y + cc
        if j < 8:
            for f, x in enumerate(rows):
                low[f, j : j + 1, :] = x
            for f, x in enumerate((a, b, c, ra, rb)):
                low[9 + f, j : j + 1, :] = x
        else:
            for f, x in enumerate(rows):
                high[f, GROUP - 1 - j : GROUP - j, :] = x
    return rows


def link_step(front, back, pk, pv):
    d, y, c = front[:3], front[3:5], front[5:]
    bd, by, bc = back[:3], back[3:5], back[5:]
    ea, eb, ec, ed = (
        bd[0] - SPRING * pk[0],
        bd[1] - SPRING * pk[1],
        bd[1] - SPRING * pk[2],
        bd[2] - SPRING * pk[3],
    )
    r = 1.0 / (ea * ed - eb * ec)
    einv = (ed * r, -eb * r, -ec * r, ea * r)
    dinv = full(inv_sym(*d))
    through = mul22(c, pk)
    lead = mul22(through, einv)
    gain = mul22(lead, bc)
    gain = (gain[0] + SPRING, gain[1], gain[2], gain[3] + SPRING)
    load = mul21(lead, (by[0] + SPRING * pv[0], by[1] + SPRING * pv[1]))
    held = mul21(c, pv)
    return mul22(dinv, gain), mul21(dinv, (y[0] + held[0] + load[0], y[1] + held[1] + load[1]))


def links(recv, group, groups, own):
    left = iota((1, 128), 1) < 64
    none = jnp.zeros((1, 128))
    pk, pv = (none,) * 4, (none,) * 2
    limit = jnp.where(left, group, groups - 1 - group)
    for j in range(groups - 1):
        here = [recv[j, f : f + 1, :] for f in range(9)]
        there = [recv[groups - 1 - j, f : f + 1, :] for f in range(9)]
        front = tuple(jnp.where(left, x, z) for x, z in zip(here, there))
        back = tuple(half_turn(jnp.where(left, z, x)) for x, z in zip(here, there))
        nk, nv = link_step(front, back, pk, pv)
        use = limit > j
        pk = tuple(jnp.where(use, n, o) for n, o in zip(nk, pk))
        pv = tuple(jnp.where(use, n, o) for n, o in zip(nv, pv))
    nk, nv = link_step(own, tuple(half_turn(x) for x in own), pk, pv)
    rk, rv = tuple(half_turn(x) for x in pk), tuple(half_turn(x) for x in pv)
    t = mul22(nk, rk)
    a, b, c, d = 1.0 - t[0], -t[1], -t[2], 1.0 - t[3]
    r = 1.0 / (a * d - b * c)
    rhs = mul21(nk, rv)
    w = mul21((d * r, -b * r, -c * r, a * r), (rhs[0] + nv[0], rhs[1] + nv[1]))
    x = mul21(rk, w)
    return half_turn(x[0] + rv[0]), half_turn(x[1] + rv[1])


def interior(low, high, bound):
    lo = [low[f] for f in range(14)]
    hi = [high[f] for f in range(9)]
    other = [half_turn(x) for x in hi[:5]]
    d = [lo[f] + other[f] - lo[9 + f] for f in range(5)]
    near = mul21(lo[5:9], bound)
    far = mul21(hi[5:9], bound)
    rhs = [d[3 + n] + near[n] + half_turn(far[n]) for n in range(2)]
    return mul21(full(inv_sym(*d[:3])), rhs)


def kernel(
    sections,
    strips,
    image,
    w1_ref,
    w2_ref,
    marks_ref,
    out_ref,
    nwin,
    owin,
    sel,
    w1b,
    w2p,
    nxs,
    oxs,
    nfm,
    ofm,
    lall,
    rall,
    scores,
    mom,
    send_a,
    recv_a,
    low,
    high,
    send_b,
    recv_b,
    send_c,
    recv_c,
    local_sem,
    isend,
    irecv,
    asend,
    arecv,
    bsend,
    brecv,
    csend,
    crecv,
):
    s, r = lax.axis_index("gz"), lax.axis_index("gy")
    groups = sections // GROUP
    group, k = lax.div(s, GROUP), lax.rem(s, GROUP)
    after, before = lax.rem(s + 1, sections), lax.rem(s + sections - 1, sections)
    down, up = lax.rem(r + 1, strips), lax.rem(r + strips - 1, strips)
    mates = [GROUP * group + lax.rem(k + o, GROUP) for o in range(GROUP)]
    peers = [GROUP * lax.rem(group + o, groups) + k for o in range(groups)]

    local = pltpu.make_async_copy(image, owin.at[pl.ds(16, 128)], local_sem)
    local.start()
    barrier = pltpu.get_barrier_semaphore()
    partners = [
        (before, r),
        (after, r),
        (before, up),
        (after, down),
        (before, down),
        (after, up),
        (s, down),
        (s, up),
    ]
    partners += [(m, r) for m in mates[1:]] + [(m, r) for m in peers[1:]]
    for place in partners:
        pl.semaphore_signal(barrier, inc=1, device_id=place, device_id_type=MESH)

    build_weights(w1_ref, w2_ref, sel, w1b, w2p)
    nxs[:, 0:16, :] = jnp.zeros((7, 16, 128), BF)
    oxs[:, 0:16, :] = jnp.zeros((7, 16, 128), BF)
    oxs[:, 160:176, :] = jnp.zeros((7, 16, 128), BF)

    pl.semaphore_wait(barrier, len(partners))

    def remote(src, dst, ssem, rsem, place):
        return pltpu.make_async_remote_copy(
            src_ref=src,
            dst_ref=dst,
            send_sem=ssem,
            recv_sem=rsem,
            device_id=place,
            device_id_type=MESH,
        )

    halo = remote(image.at[pl.ds(112, 16)], owin.at[pl.ds(0, 16)], isend.at[0], irecv.at[0], (s, down))
    moves = [
        remote(image, nwin.at[pl.ds(32, 128)], isend.at[1], irecv.at[1], (before, r)),
        remote(
            image.at[pl.ds(96, 32)], nwin.at[pl.ds(0, 32)], isend.at[2], irecv.at[2], (before, down)
        ),
        remote(
            image.at[pl.ds(0, 32)], nwin.at[pl.ds(160, 32)], isend.at[3], irecv.at[3], (before, up)
        ),
    ]
    halo.start()
    for move in moves:
        move.start()
    local.wait()
    halo.wait()

    @pl.when(r == 0)
    def _():
        owin[0:16, :] = jnp.zeros((16, 512), BF)

    split_columns(owin, 144, sel, oxs)

    def loop(count, step):
        def run(i, carry):
            step(i)
            return carry

        lax.fori_loop(0, count, run, 0)

    loop(5, lambda i: conv_rows(oxs, w1b, ofm, 5, i))
    loop(16, lambda i: own_pair(ofm, w2p, rall, i))

    for move in moves:
        move.wait()

    @pl.when(r == 0)
    def _():
        nwin[0:32, :] = jnp.zeros((32, 512), BF)

    @pl.when(r == strips - 1)
    def _():
        nwin[160:192, :] = jnp.zeros((32, 512), BF)

    split_columns(nwin, 192, sel, nxs)
    loop(6, lambda i: conv_rows(nxs, w1b, nfm, 6, i))
    loop(11, lambda i: next_group(nfm, w2p, lall, 32 * r - 6, i))
    loop(16, lambda i: correlate_pair(lall, rall, scores, mom, i))

    node_blocks(mom, marks_ref, s == sections - 1, send_a)
    moves_a = [
        remote(send_a.at[mates[o]  - GROUP * group], recv_a.at[k], asend.at[o - 1], arecv.at[o - 1], (mates[o], r))
        for o in range(1, GROUP)
    ]
    for move in moves_a:
        move.start()
    recv_a[k] = send_a[k]
    for move in moves_a:
        move.wait()

    ends = segment(recv_a, group, sections, low, high)
    for f, x in enumerate(ends):
        send_b[f : f + 1, :] = x
    moves_b = [
        remote(send_b, recv_b.at[group], bsend.at[o - 1], brecv.at[o - 1], (peers[o], r))
        for o in range(1, groups)
    ]
    for move in moves_b:
        move.start()
    recv_b[group] = send_b[...]
    for move in moves_b:
        move.wait()

    bound = links(recv_b, group, groups, ends)
    xa, xb = interior(low, high, bound)
    left8 = iota((8, 128), 1) < 64
    front = jnp.where(left8, xa, half_turn(xb))
    rear = jnp.where(left8, half_turn(xa), xb)
    for j in range(8):
        send_c[j] = front[j : j + 1]
        send_c[GROUP - 1 - j] = rear[j : j + 1]
    slot = 8 * lax.rem(k, 2) + lax.div(k, 2)
    moves_c = [
        remote(send_c.at[mates[o] - GROUP * group], recv_c.at[slot], csend.at[o - 1], crecv.at[o - 1], (mates[o], r))
        for o in range(1, GROUP)
    ]
    for move in moves_c:
        move.start()
    recv_c[slot] = send_c[k]
    for move in moves_c:
        move.wait()
    even = jnp.concatenate([recv_c[q] for q in range(8)], axis=0)
    odd = jnp.concatenate([recv_c[q] for q in range(8, 16)], axis=0)
    out_ref[0] = jnp.where(left8, even, half_turn(odd))
    out_ref[1] = jnp.where(left8, half_turn(even), odd)


def body(sections, strips, image, conv_one, conv_two, tissue):
    groups = sections // GROUP
    vmem = pl.BlockSpec(memory_space=pltpu.VMEM)
    dma = pltpu.SemaphoreType.DMA
    out = pl.pallas_call(
        lambda *refs: kernel(sections, strips, *refs),
        out_shape=jax.ShapeDtypeStruct((2, 8, 128), F32),
        in_specs=[pl.BlockSpec(memory_space=pl.ANY), vmem, vmem, vmem],
        out_specs=vmem,
        scratch_shapes=[
            pltpu.VMEM((192, 512), BF),
            pltpu.VMEM((144, 512), BF),
            pltpu.VMEM((512, 896), BF),
            pltpu.VMEM((384, 224), BF),
            pltpu.VMEM((32, 144), BF),
            pltpu.VMEM((7, 208, 128), BF),
            pltpu.VMEM((7, 176, 128), BF),
            pltpu.VMEM((12 * 384, 128), BF),
            pltpu.VMEM((10 * 384, 128), BF),
            pltpu.VMEM((44 * ROWS, 256), BF),
            pltpu.VMEM((16, 256, 256), BF),
            pltpu.VMEM((14 * ROWS, 256), F32),
            pltpu.VMEM((16, 8, 256), F32),
            pltpu.VMEM((GROUP, 5, 128), F32),
            pltpu.VMEM((GROUP, 5, 128), F32),
            pltpu.VMEM((14, 8, 128), F32),
            pltpu.VMEM((9, 8, 128), F32),
            pltpu.VMEM((9, 128), F32),
            pltpu.VMEM((groups, 9, 128), F32),
            pltpu.VMEM((GROUP, 1, 128), F32),
            pltpu.VMEM((GROUP, 1, 128), F32),
            dma,
            dma((4,)),
            dma((4,)),
            dma((GROUP - 1,)),
            dma((GROUP - 1,)),
            dma((groups - 1,)),
            dma((groups - 1,)),
            dma((GROUP - 1,)),
            dma((GROUP - 1,)),
        ],
        compiler_params=pltpu.CompilerParams(
            collective_id=0, has_side_effects=True, vmem_limit_bytes=32 * 1024 * 1024
        ),
    )(image.reshape(128, 512), conv_one, conv_two, tissue.reshape(8, 128))
    return out.reshape(2, 1, 1024)


def solution(mesh):
    sections, strips = mesh.shape["gz"], mesh.shape["gy"]
    placed = (P("gz", "gy", None), P(), P(), P("gz", "gy"))
    return jax.shard_map(
        lambda *args: body(sections, strips, *args),
        mesh=mesh,
        in_specs=placed,
        out_specs=P(None, "gz", "gy"),
        check_vma=False,
    )
```

```python
import jax
import jax.numpy as jnp
from jax import lax
from jax.experimental import pallas as pl
from jax.experimental.pallas import tpu as pltpu
from jax.sharding import PartitionSpec as P

BF, F32 = jnp.bfloat16, jnp.float32
MESH = pl.DeviceIdType.MESH
GROUP = 16
SPRING, ANCHOR = 8.0, 0.02
PARTS = 2
VMEM_LIMIT = 60 * 1024 * 1024
ROWS = 32
SCALE = 32 ** (-0.5) * 1.4426950408889634


def iota(shape, dim):
    return lax.broadcasted_iota(jnp.int32, shape, dim)


def mm(left, right):
    return jnp.dot(left, right, preferred_element_type=F32)


def far_first(count):
    return sorted(range(1, count), key=lambda o: -min(o, count - o))


def half_turn(x):
    return pltpu.roll(x, 64, 1)


def inv_sym(a, b, c):
    r = 1.0 / (a * c - b * b)
    return c * r, -b * r, a * r


def mul22(l, r):
    return (
        l[0] * r[0] + l[1] * r[2],
        l[0] * r[1] + l[1] * r[3],
        l[2] * r[0] + l[3] * r[2],
        l[2] * r[1] + l[3] * r[3],
    )


def mul21(l, v):
    return l[0] * v[0] + l[1] * v[1], l[2] * v[0] + l[3] * v[1]


def full(sym):
    return sym[0], sym[1], sym[1], sym[2]


def build_weights(w1_ref, w2_ref, sel, w1b, w2p):
    col = iota((256, 256), 1)
    sel[...] = jnp.where(iota((256, 256), 0) == 4 * (col & 63) + (col >> 6), 1.0, 0.0).astype(BF)
    tap, col = iota((9, 256), 0), iota((9, 256), 1)
    a = (tap * 11) >> 5
    da = (col & 31) - 15 - a
    db = (col >> 5) - (tap - 3 * a)
    w1 = w1_ref[...]
    base = jnp.concatenate(
        [mm(w1, jnp.where((da == 0) & (db == 2 * b), 1.0, 0.0).astype(BF)) for b in range(3)], axis=0
    )
    for f in range(8):
        moved = base if f == 0 else pltpu.roll(base, 2 * f, 1)
        w1b[48 * f : 48 * f + 48, :] = moved[:, :224].astype(BF)
    k, n = iota((144, 144), 0), iota((144, 144), 1)
    ab = n >> 4
    perm = jnp.where(k == 9 * (n & 15) + ab, 1.0, 0.0).astype(BF)
    w2p[...] = mm(w2_ref[...], perm).astype(BF)


def split_columns(window, low, rows, sel, xs):
    span = slice(16 + low, 16 + low + rows)
    out = [mm(window[low : low + rows, 256 * h : 256 * h + 256], sel[...]) for h in range(2)]
    lane = iota((rows, 128), 1)
    for n in range(2):
        one, two = (x[:, 128 * n : 128 * n + 128] for x in out)
        even = jnp.where(lane < 64, one, half_turn(two))
        odd = jnp.where(lane < 64, half_turn(one), two)
        for phase, x in ((2 * n, even), (2 * n + 1, odd)):
            xs[phase + 3, span, :] = x.astype(BF)
            if phase > 0:
                xs[phase - 1, span, :] = jnp.where(lane == 0, 0.0, pltpu.roll(x, 1, 1)).astype(BF)


def conv_rows(xs, w1b, fm, half, low):
    def column(block):
        start = 16 * block if isinstance(block, int) else pl.multiple_of(16 * block, 16)
        return jnp.concatenate([xs[v, pl.ds(start, 32), :] for v in range(7)], axis=0)

    right = jnp.concatenate([column(low), column(low + half)], axis=1)
    out = jnp.maximum(mm(w1b[...], right), 0.0).astype(BF)
    for n in range(2):
        start = 384 * (low + n * half)
        start = start if isinstance(low, int) else pl.multiple_of(start, 128)
        fm[pl.ds(start, 384), :] = out[:, 128 * n : 128 * n + 128]


def conv_features(fm, w2p, first, count):
    starts = [96 * (first + q) - 48 for q in range(count)]
    if not isinstance(first, int):
        starts = [pl.multiple_of(x, 16) for x in starts]
    right = jnp.concatenate([fm[pl.ds(x, 144), :] for x in starts], axis=1)
    return jnp.maximum(mm(w2p[...], right), 0.0).astype(BF).astype(F32)


def own_pair(fm, w2p, rall, p):
    feats = conv_features(fm, w2p, 4 + 2 * p, 2)
    chunk = (iota((32, 256), 1) & 127) >> 4
    rall[p] = jnp.concatenate(
        [jnp.where(chunk == m, feats, 0.0) for m in range(8)], axis=0
    ).astype(BF)


def next_group(fm, w2p, lall, row_base, g):
    feats = conv_features(fm, w2p, 4 * g + 2, 4)
    stack = jnp.concatenate(
        [
            feats[:, 128 * q : 128 * q + 128] * (row_base + 4 * g + q < 128).astype(F32)
            for q in range(4)
        ],
        axis=0,
    )
    stack = stack.astype(BF)
    spun = jnp.concatenate([stack] + [jnp.concatenate([stack[128 - 32 * k :], stack[: 128 - 32 * k]], axis=0) for k in range(1, 4)], axis=0)
    place = jnp.where(iota((144, 128), 0) == iota((144, 128), 1) + 6, 1.0, 0.0).astype(BF)
    turned = lax.dot_general(place, spun, (((1,), (1,)), ((), ())), preferred_element_type=F32)
    rot = [turned[:, 128 * k : 128 * k + 128] for k in range(4)]
    lane = iota((32, 128), 1) >> 5
    for q in range(4):
        halves = []
        for h in range(2):
            pick = [rot[(g4 - q) % 4][64 * h + 16 * g4 : 64 * h + 16 * g4 + 32] for g4 in range(4)]
            halves.append(
                jnp.where(
                    lane < 2,
                    jnp.where(lane == 0, pick[0], pick[1]),
                    jnp.where(lane == 2, pick[2], pick[3]),
                )
            )
        lall[128 * g + 32 * q : 128 * g + 32 * q + 32, :] = jnp.concatenate(
            halves, axis=1
        ).astype(BF)


def score_part(lall, rall, scores, p, part, parts):
    rows = 14 * ROWS // parts
    left = lall[pl.ds(pl.multiple_of(64 * p + rows * part, 16), rows), :]
    scores[rows * part : rows * part + rows, :] = mm(left, rall[p])


def moments_pair(scores, mom, p, between):
    shift = iota((ROWS, 128), 0) - (iota((ROWS, 128), 1) & 15)
    valid = (shift >= 0) & (shift <= 12)
    b = (shift - 6).astype(F32)
    for par in range(2):
        cols = slice(128 * par, 128 * par + 128)

        def at(n):
            return scores[ROWS * (n + par) : ROWS * (n + par) + ROWS, cols]

        between(2 * par)
        high = at(0)
        for n in range(1, 13):
            high = jnp.maximum(high, at(n))
        top = jnp.max(jnp.where(valid, high, -3e38), axis=0, keepdims=True)
        between(2 * par + 1)
        t0 = t1 = t2 = None
        for n in range(12, -1, -1):
            e = jnp.exp2((at(n) - top) * SCALE)
            t0 = e if t0 is None else t0 + e
            t1 = t0 if t1 is None else t1 + t0
            t2 = t1 if t2 is None else t2 + t1
        t0 = jnp.where(valid, t0, 0.0)
        t1 = jnp.where(valid, t1, 0.0)
        t2 = jnp.where(valid, t2, 0.0)
        tb = t0 * b
        for field, term in enumerate((t0, t1, t2, tb, tb * b, t1 * b)):
            mom[p, field : field + 1, cols] = jnp.sum(term, axis=0, keepdims=True)


def node_blocks(mom, marks_ref, last, send):
    m0, m1, m2, mb, mbb, mab = (mom[:, f, :] for f in range(6))
    r = 1.0 / m0
    n1, mean_b = m1 * r, mb * r
    mean_a = n1 - 7.0
    var_a = (2.0 * m2 - 15.0 * m1) * r + 49.0 - mean_a * mean_a + 1.0
    var_b = mbb * r - mean_b * mean_b + 1.0
    cov = mab * r - n1 * mean_b
    i_aa, i_ab, i_bb = inv_sym(var_a, cov, var_b)
    p_a = i_aa * mean_a + i_ab * mean_b
    p_b = i_ab * mean_a + i_bb * mean_b
    stack = jnp.concatenate([x[:, :128] + x[:, 128:] for x in (i_aa, i_ab, i_bb, p_a, p_b)], axis=0)
    pool = jnp.where((iota((128, 128), 0) >> 1) == (iota((128, 128), 1) & 63), 0.25, 0.0)
    pooled = jnp.dot(stack, pool, precision=lax.Precision.HIGHEST, preferred_element_type=F32)
    spread = jnp.where((iota((16, 8), 0) >> 1) == iota((16, 8), 1), 1.0, 0.0)
    marks = mm(spread, marks_ref[...].astype(F32))
    same = (iota((16, 128), 0) & 1) == (iota((16, 128), 1) >> 6)
    marks = jnp.where(same, marks, half_turn(marks)) * jnp.where(last, 0.0, 1.0)
    for f in range(5):
        data = pooled[16 * f : 16 * f + 16] * marks
        for q in range(16):
            send[q, f : f + 1, :] = data[q : q + 1]


def segment(recv, group, sections, low, high):
    left = iota((1, 128), 1) < 64
    first = None
    for j in range(GROUP):
        a, b, c, ra, rb = (
            jnp.where(left, recv[j, f : f + 1, :], recv[GROUP - 1 - j, f : f + 1, :]) for f in range(5)
        )
        section = GROUP * group + jnp.where(left, j, GROUP - 1 - j)
        ends = (section == 0) | (section == sections - 1)
        extra = jnp.where(ends, SPRING + ANCHOR, 2 * SPRING + ANCHOR)
        a, c = a + extra, c + extra
        if j == 0:
            d, y = (a, b, c), (ra, rb)
            eight, none = jnp.full((1, 128), SPRING), jnp.zeros((1, 128))
            cc = (eight, none, none, eight)
        else:
            inv = tuple(SPRING * x for x in inv_sym(*d))
            iy = mul21(full(inv), y)
            d = (a - SPRING * inv[0], b - SPRING * inv[1], c - SPRING * inv[2])
            y = (ra + iy[0], rb + iy[1])
            cc = mul22(full(inv), cc)
        rows = d + y + cc
        if j < 8:
            for f, x in enumerate(rows):
                low[f, j : j + 1, :] = x
            for f, x in enumerate((a, b, c, ra, rb)):
                low[9 + f, j : j + 1, :] = x
        else:
            for f, x in enumerate(rows):
                high[f, GROUP - 1 - j : GROUP - j, :] = x
    return rows


def link_step(front, back, pk, pv):
    d, y, c = front[:3], front[3:5], front[5:]
    bd, by, bc = back[:3], back[3:5], back[5:]
    ea, eb, ec, ed = (
        bd[0] - SPRING * pk[0],
        bd[1] - SPRING * pk[1],
        bd[1] - SPRING * pk[2],
        bd[2] - SPRING * pk[3],
    )
    r = 1.0 / (ea * ed - eb * ec)
    einv = (ed * r, -eb * r, -ec * r, ea * r)
    dinv = full(inv_sym(*d))
    through = mul22(c, pk)
    lead = mul22(through, einv)
    gain = mul22(lead, bc)
    gain = (gain[0] + SPRING, gain[1], gain[2], gain[3] + SPRING)
    load = mul21(lead, (by[0] + SPRING * pv[0], by[1] + SPRING * pv[1]))
    held = mul21(c, pv)
    return mul22(dinv, gain), mul21(dinv, (y[0] + held[0] + load[0], y[1] + held[1] + load[1]))


def links(recv, group, groups, own):
    left = iota((1, 128), 1) < 64
    none = jnp.zeros((1, 128))
    pk, pv = (none,) * 4, (none,) * 2
    limit = jnp.where(left, group, groups - 1 - group)
    for j in range(groups - 1):
        here = [recv[j, f : f + 1, :] for f in range(9)]
        there = [recv[groups - 1 - j, f : f + 1, :] for f in range(9)]
        front = tuple(jnp.where(left, x, z) for x, z in zip(here, there))
        back = tuple(half_turn(jnp.where(left, z, x)) for x, z in zip(here, there))
        nk, nv = link_step(front, back, pk, pv)
        use = limit > j
        pk = tuple(jnp.where(use, n, o) for n, o in zip(nk, pk))
        pv = tuple(jnp.where(use, n, o) for n, o in zip(nv, pv))
    nk, nv = link_step(own, tuple(half_turn(x) for x in own), pk, pv)
    rk, rv = tuple(half_turn(x) for x in pk), tuple(half_turn(x) for x in pv)
    t = mul22(nk, rk)
    a, b, c, d = 1.0 - t[0], -t[1], -t[2], 1.0 - t[3]
    r = 1.0 / (a * d - b * c)
    rhs = mul21(nk, rv)
    w = mul21((d * r, -b * r, -c * r, a * r), (rhs[0] + nv[0], rhs[1] + nv[1]))
    x = mul21(rk, w)
    return half_turn(x[0] + rv[0]), half_turn(x[1] + rv[1])


def interior(low, high, bound):
    lo = [low[f] for f in range(14)]
    hi = [high[f] for f in range(9)]
    other = [half_turn(x) for x in hi[:5]]
    d = [lo[f] + other[f] - lo[9 + f] for f in range(5)]
    near = mul21(lo[5:9], bound)
    far = mul21(hi[5:9], bound)
    rhs = [d[3 + n] + near[n] + half_turn(far[n]) for n in range(2)]
    return mul21(full(inv_sym(*d[:3])), rhs)


def kernel(
    sections,
    strips,
    image,
    w1_hbm,
    w2_hbm,
    marks_hbm,
    out_ref,
    w1_ref,
    w2_ref,
    marks_ref,
    nwin,
    owin,
    sel,
    w1b,
    w2p,
    nxs,
    oxs,
    nfm,
    ofm,
    lall,
    rall,
    scores_a,
    scores_b,
    mom,
    send_a,
    recv_a,
    low,
    high,
    send_b,
    recv_b,
    send_c,
    recv_c,
    local_sem,
    isend,
    irecv,
    asend,
    arecv,
    bsend,
    brecv,
    csend,
    crecv,
):
    s, r = lax.axis_index("gz"), lax.axis_index("gy")
    groups = sections // GROUP
    group, k = lax.div(s, GROUP), lax.rem(s, GROUP)
    after, before = lax.rem(s + 1, sections), lax.rem(s + sections - 1, sections)
    down, up = lax.rem(r + 1, strips), lax.rem(r + strips - 1, strips)
    mates = [GROUP * group + lax.rem(k + o, GROUP) for o in range(GROUP)]
    peers = [GROUP * lax.rem(group + o, groups) + k for o in range(groups)]

    local = pltpu.make_async_copy(image, owin.at[pl.ds(16, 128)], local_sem.at[0])
    smalls = [
        pltpu.make_async_copy(src, dst, local_sem.at[n + 1])
        for n, (src, dst) in enumerate(((w1_hbm, w1_ref), (w2_hbm, w2_ref), (marks_hbm, marks_ref)))
    ]
    for move in smalls:
        move.start()
    local.start()
    barrier = pltpu.get_barrier_semaphore()
    partners = [
        (before, r),
        (after, r),
        (before, up),
        (after, down),
        (before, down),
        (after, up),
        (s, down),
        (s, up),
    ]
    partners += [(m, r) for m in mates[1:]] + [(m, r) for m in peers[1:]]
    for place in partners:
        pl.semaphore_signal(barrier, inc=1, device_id=place, device_id_type=MESH)

    for move in smalls:
        move.wait()
    build_weights(w1_ref, w2_ref, sel, w1b, w2p)
    nxs[:, 0:16, :] = jnp.zeros((7, 16, 128), BF)
    oxs[:, 0:16, :] = jnp.zeros((7, 16, 128), BF)
    oxs[:, 160:176, :] = jnp.zeros((7, 16, 128), BF)

    pl.semaphore_wait(barrier, len(partners))

    def remote(src, dst, ssem, rsem, place):
        return pltpu.make_async_remote_copy(
            src_ref=src,
            dst_ref=dst,
            send_sem=ssem,
            recv_sem=rsem,
            device_id=place,
            device_id_type=MESH,
        )

    halo = remote(image.at[pl.ds(112, 16)], owin.at[pl.ds(0, 16)], isend.at[0], irecv.at[0], (s, down))
    def piece(row, target, n, place):
        return remote(
            image.at[pl.ds(row, 32)], nwin.at[pl.ds(target, 32)], isend.at[n], irecv.at[n], place
        )

    moves = [piece(96, 0, 1, (before, down))]
    moves += [piece(32 * c, 32 + 32 * c, 2 + c, (before, r)) for c in range(4)]
    moves += [piece(0, 160, 6, (before, up))]
    halo.start()
    for move in (moves[0], moves[5], *moves[1:5]):
        move.start()
    local.wait()

    def loop(low, high, step):
        def run(i, carry):
            step(i)
            return carry

        lax.fori_loop(low, high, run, 0)

    split_columns(owin, 16, 128, sel, oxs)
    loop(2, 5, lambda i: conv_rows(oxs, w1b, ofm, 3, i))
    conv_rows(oxs, w1b, ofm, 1, 8)
    loop(3, 16, lambda i: own_pair(ofm, w2p, rall, i))
    halo.wait_recv()

    @pl.when(r == 0)
    def _():
        owin[0:16, :] = jnp.zeros((16, 512), BF)

    split_columns(owin, 0, 16, sel, oxs)
    conv_rows(oxs, w1b, ofm, 1, 0)
    for p in range(3):
        own_pair(ofm, w2p, rall, p)

    for half in range(2):
        for c in range(3):
            moves[3 * half + c].wait_recv()
        edge = 160 * half

        @pl.when(r == (strips - 1) * half)
        def _():
            nwin[edge : edge + 32, :] = jnp.zeros((32, 512), BF)

        split_columns(nwin, 96 * half, 96, sel, nxs)
        block = 6 * half
        conv_rows(nxs, w1b, nfm, 1, block)
        conv_rows(nxs, w1b, nfm, 1, block + 2)
        for g in (0,) if half == 0 else (5, 6):
            next_group(nfm, w2p, lall, 32 * r - 6, g)
        conv_rows(nxs, w1b, nfm, 1, block + 4)
        for g in range(1, 5) if half == 0 else range(7, 11):
            next_group(nfm, w2p, lall, 32 * r - 6, g)

    score_part(lall, rall, scores_a, 0, 0, 1)

    def two_pairs(i):
        for now, later, p in ((scores_a, scores_b, 2 * i), (scores_b, scores_a, 2 * i + 1)):
            q = jnp.minimum(p + 1, 15)

            def ahead(n):
                if n % (4 // PARTS) == 0:
                    score_part(lall, rall, later, q, n // (4 // PARTS), PARTS)

            moments_pair(now, mom, p, ahead)

    loop(0, 8, two_pairs)

    node_blocks(mom, marks_ref, s == sections - 1, send_a)
    moves_a = [
        remote(send_a.at[mates[o]  - GROUP * group], recv_a.at[k], asend.at[o - 1], arecv.at[o - 1], (mates[o], r))
        for o in far_first(GROUP)
    ]
    for move in moves_a:
        move.start()
    recv_a[k] = send_a[k]
    for move in moves_a:
        move.wait_recv()

    ends = segment(recv_a, group, sections, low, high)
    for f, x in enumerate(ends):
        send_b[f : f + 1, :] = x
    moves_b = [
        remote(send_b, recv_b.at[group], bsend.at[o - 1], brecv.at[o - 1], (peers[o], r))
        for o in far_first(groups)
    ]
    for move in moves_b:
        move.start()
    recv_b[group] = send_b[...]
    for move in moves_b:
        move.wait_recv()

    bound = links(recv_b, group, groups, ends)
    xa, xb = interior(low, high, bound)
    left8 = iota((8, 128), 1) < 64
    front = jnp.where(left8, xa, half_turn(xb))
    rear = jnp.where(left8, half_turn(xa), xb)
    for j in range(8):
        send_c[j] = front[j : j + 1]
        send_c[GROUP - 1 - j] = rear[j : j + 1]
    slot = 8 * lax.rem(k, 2) + lax.div(k, 2)
    moves_c = [
        remote(send_c.at[mates[o] - GROUP * group], recv_c.at[slot], csend.at[o - 1], crecv.at[o - 1], (mates[o], r))
        for o in far_first(GROUP)
    ]
    for move in moves_c:
        move.start()
    recv_c[slot] = send_c[k]
    for move in moves_c:
        move.wait_recv()
    even = jnp.concatenate([recv_c[q] for q in range(8)], axis=0)
    odd = jnp.concatenate([recv_c[q] for q in range(8, 16)], axis=0)
    out_ref[0] = jnp.where(left8, even, half_turn(odd))
    out_ref[1] = jnp.where(left8, half_turn(even), odd)
    for move in (halo, *moves, *moves_a, *moves_b, *moves_c):
        move.wait_send()


def body(sections, strips, image, conv_one, conv_two, tissue):
    groups = sections // GROUP
    vmem = pl.BlockSpec(memory_space=pltpu.VMEM)
    dma = pltpu.SemaphoreType.DMA
    out = pl.pallas_call(
        lambda *refs: kernel(sections, strips, *refs),
        out_shape=jax.ShapeDtypeStruct((2, 8, 128), F32),
        in_specs=[pl.BlockSpec(memory_space=pl.ANY)] * 4,
        out_specs=vmem,
        scratch_shapes=[
            pltpu.VMEM((16, 9), BF),
            pltpu.VMEM((32, 144), BF),
            pltpu.VMEM((8, 128), jnp.int32),
            pltpu.VMEM((192, 512), BF),
            pltpu.VMEM((144, 512), BF),
            pltpu.VMEM((256, 256), BF),
            pltpu.VMEM((384, 224), BF),
            pltpu.VMEM((32, 144), BF),
            pltpu.VMEM((7, 208, 128), BF),
            pltpu.VMEM((7, 176, 128), BF),
            pltpu.VMEM((12 * 384, 128), BF),
            pltpu.VMEM((10 * 384, 128), BF),
            pltpu.VMEM((44 * ROWS, 256), BF),
            pltpu.VMEM((16, 256, 256), BF),
            pltpu.VMEM((14 * ROWS, 256), F32),
            pltpu.VMEM((14 * ROWS, 256), F32),
            pltpu.VMEM((16, 8, 256), F32),
            pltpu.VMEM((GROUP, 5, 128), F32),
            pltpu.VMEM((GROUP, 5, 128), F32),
            pltpu.VMEM((14, 8, 128), F32),
            pltpu.VMEM((9, 8, 128), F32),
            pltpu.VMEM((9, 128), F32),
            pltpu.VMEM((groups, 9, 128), F32),
            pltpu.VMEM((GROUP, 1, 128), F32),
            pltpu.VMEM((GROUP, 1, 128), F32),
            dma((4,)),
            dma((7,)),
            dma((7,)),
            dma((GROUP - 1,)),
            dma((GROUP - 1,)),
            dma((groups - 1,)),
            dma((groups - 1,)),
            dma((GROUP - 1,)),
            dma((GROUP - 1,)),
        ],
        compiler_params=pltpu.CompilerParams(
            collective_id=0, has_side_effects=True, vmem_limit_bytes=VMEM_LIMIT
        ),
    )(image.reshape(128, 512), conv_one, conv_two, tissue.reshape(8, 128))
    return out.reshape(2, 1, 1024)


def solution(mesh):
    sections, strips = mesh.shape["gz"], mesh.shape["gy"]
    placed = (P("gz", "gy", None), P(), P(), P("gz", "gy"))
    return jax.shard_map(
        lambda *args: body(sections, strips, *args),
        mesh=mesh,
        in_specs=placed,
        out_specs=P(None, "gz", "gy"),
        check_vma=False,
    )
```

```python
import jax
import jax.numpy as jnp
from jax import lax
from jax.experimental import pallas as pl
from jax.experimental.pallas import tpu as pltpu
from jax.sharding import PartitionSpec as P

BF, F32 = jnp.bfloat16, jnp.float32
MESH = pl.DeviceIdType.MESH
GROUP = 16
SPRING, ANCHOR = 8.0, 0.02
AHEAD, BUFFERS = 3, 4
VMEM_LIMIT = 60 * 1024 * 1024
ROWS = 32
SCALE = 32 ** (-0.5) * 1.4426950408889634


def iota(shape, dim):
    return lax.broadcasted_iota(jnp.int32, shape, dim)


def mm(left, right):
    return jnp.dot(left, right, preferred_element_type=F32)


def far_first(count):
    return sorted(range(1, count), key=lambda o: -min(o, count - o))


def half_turn(x):
    return pltpu.roll(x, 64, 1)


def inv_sym(a, b, c):
    r = 1.0 / (a * c - b * b)
    return c * r, -b * r, a * r


def mul22(l, r):
    return (
        l[0] * r[0] + l[1] * r[2],
        l[0] * r[1] + l[1] * r[3],
        l[2] * r[0] + l[3] * r[2],
        l[2] * r[1] + l[3] * r[3],
    )


def mul21(l, v):
    return l[0] * v[0] + l[1] * v[1], l[2] * v[0] + l[3] * v[1]


def full(sym):
    return sym[0], sym[1], sym[1], sym[2]


def build_weights(w1_ref, w2_ref, sel, w1b, w2p):
    col = iota((256, 256), 1)
    sel[...] = jnp.where(iota((256, 256), 0) == 4 * (col & 63) + (col >> 6), 1.0, 0.0).astype(BF)
    tap, col = iota((9, 256), 0), iota((9, 256), 1)
    a = (tap * 11) >> 5
    da = (col & 31) - 15 - a
    db = (col >> 5) - (tap - 3 * a)
    w1 = w1_ref[...]
    base = jnp.concatenate(
        [mm(w1, jnp.where((da == 0) & (db == 2 * b), 1.0, 0.0).astype(BF)) for b in range(3)], axis=0
    )
    for f in range(8):
        moved = base if f == 0 else pltpu.roll(base, 2 * f, 1)
        w1b[48 * f : 48 * f + 48, :] = moved[:, :224].astype(BF)
    k, n = iota((144, 144), 0), iota((144, 144), 1)
    ab = n >> 4
    perm = jnp.where(k == 9 * (n & 15) + ab, 1.0, 0.0).astype(BF)
    w2p[...] = mm(w2_ref[...], perm).astype(BF)


def split_columns(window, low, rows, sel, xs):
    span = slice(16 + low, 16 + low + rows)
    out = [mm(window[low : low + rows, 256 * h : 256 * h + 256], sel[...]) for h in range(2)]
    lane = iota((rows, 128), 1)
    for n in range(2):
        one, two = (x[:, 128 * n : 128 * n + 128] for x in out)
        even = jnp.where(lane < 64, one, half_turn(two))
        odd = jnp.where(lane < 64, half_turn(one), two)
        for phase, x in ((2 * n, even), (2 * n + 1, odd)):
            xs[phase + 3, span, :] = x.astype(BF)
            if phase > 0:
                xs[phase - 1, span, :] = jnp.where(lane == 0, 0.0, pltpu.roll(x, 1, 1)).astype(BF)


def conv_rows(xs, w1b, fm, half, low):
    def column(block):
        start = 16 * block if isinstance(block, int) else pl.multiple_of(16 * block, 16)
        return jnp.concatenate([xs[v, pl.ds(start, 32), :] for v in range(7)], axis=0)

    right = jnp.concatenate([column(low), column(low + half)], axis=1)
    out = jnp.maximum(mm(w1b[...], right), 0.0).astype(BF)
    for n in range(2):
        start = 384 * (low + n * half)
        start = start if isinstance(low, int) else pl.multiple_of(start, 128)
        fm[pl.ds(start, 384), :] = out[:, 128 * n : 128 * n + 128]


def conv_features(fm, w2p, first, count):
    starts = [96 * (first + q) - 48 for q in range(count)]
    if not isinstance(first, int):
        starts = [pl.multiple_of(x, 16) for x in starts]
    right = jnp.concatenate([fm[pl.ds(x, 144), :] for x in starts], axis=1)
    return jnp.maximum(mm(w2p[...], right), 0.0).astype(BF).astype(F32)


def own_pair(fm, w2p, rall, p):
    feats = conv_features(fm, w2p, 4 + 2 * p, 2)
    chunk = (iota((32, 256), 1) & 127) >> 4
    rall[p] = jnp.concatenate(
        [jnp.where(chunk == m, feats, 0.0) for m in range(8)], axis=0
    ).astype(BF)


def next_group(fm, w2p, lall, row_base, g):
    feats = conv_features(fm, w2p, 4 * g + 2, 4)
    stack = jnp.concatenate(
        [
            feats[:, 128 * q : 128 * q + 128] * (row_base + 4 * g + q < 128).astype(F32)
            for q in range(4)
        ],
        axis=0,
    )
    stack = stack.astype(BF)
    place = jnp.where(iota((144, 128), 0) == iota((144, 128), 1) + 6, 1.0, 0.0).astype(BF)
    ext = lax.dot_general(place, stack, (((1,), (1,)), ((), ())), preferred_element_type=F32)
    rot = [ext] + [pltpu.roll(ext, 32 * k, 1) for k in range(1, 4)]
    lane = iota((32, 128), 1) >> 5
    for q in range(4):
        halves = []
        for h in range(2):
            pick = [rot[(g4 - q) % 4][64 * h + 16 * g4 : 64 * h + 16 * g4 + 32] for g4 in range(4)]
            halves.append(
                jnp.where(
                    lane < 2,
                    jnp.where(lane == 0, pick[0], pick[1]),
                    jnp.where(lane == 2, pick[2], pick[3]),
                )
            )
        lall[128 * g + 32 * q : 128 * g + 32 * q + 32, :] = jnp.concatenate(
            halves, axis=1
        ).astype(BF)


def score_pair(lall, rall, scores, p):
    scores[p % BUFFERS] = mm(lall[64 * p : 64 * p + 14 * ROWS, :], rall[p])


def moments_pair(scores, mom, p):
    shift = iota((ROWS, 128), 0) - (iota((ROWS, 128), 1) & 15)
    valid = (shift >= 0) & (shift <= 12)
    b = (shift - 6).astype(F32)
    for par in range(2):
        cols = slice(128 * par, 128 * par + 128)

        def at(n):
            return scores[ROWS * (n + par) : ROWS * (n + par) + ROWS, cols]

        high = at(0)
        for n in range(1, 13):
            high = jnp.maximum(high, at(n))
        top = jnp.max(jnp.where(valid, high, -3e38), axis=0, keepdims=True)
        t0 = t1 = t2 = None
        for n in range(12, -1, -1):
            e = jnp.exp2((at(n) - top) * SCALE)
            t0 = e if t0 is None else t0 + e
            t1 = t0 if t1 is None else t1 + t0
            t2 = t1 if t2 is None else t2 + t1
        t0 = jnp.where(valid, t0, 0.0)
        t1 = jnp.where(valid, t1, 0.0)
        t2 = jnp.where(valid, t2, 0.0)
        tb = t0 * b
        for field, term in enumerate((t0, t1, t2, tb, tb * b, t1 * b)):
            mom[p, field : field + 1, cols] = jnp.sum(term, axis=0, keepdims=True)


def node_marks(marks_ref, last, keep):
    spread = jnp.where((iota((16, 8), 0) >> 1) == iota((16, 8), 1), 1.0, 0.0)
    marks = mm(spread, marks_ref[...].astype(F32))
    same = (iota((16, 128), 0) & 1) == (iota((16, 128), 1) >> 6)
    keep[...] = jnp.where(same, marks, half_turn(marks)) * jnp.where(last, 0.0, 1.0)


def node_blocks(mom, keep, send):
    m0, m1, m2, mb, mbb, mab = (mom[:, f, :] for f in range(6))
    r = 1.0 / m0
    n1, mean_b = m1 * r, mb * r
    mean_a = n1 - 7.0
    var_a = (2.0 * m2 - 15.0 * m1) * r + 49.0 - mean_a * mean_a + 1.0
    var_b = mbb * r - mean_b * mean_b + 1.0
    cov = mab * r - n1 * mean_b
    i_aa, i_ab, i_bb = inv_sym(var_a, cov, var_b)
    p_a = i_aa * mean_a + i_ab * mean_b
    p_b = i_ab * mean_a + i_bb * mean_b
    stack = jnp.concatenate([x[:, :128] + x[:, 128:] for x in (i_aa, i_ab, i_bb, p_a, p_b)], axis=0)
    pool = jnp.where((iota((128, 128), 0) >> 1) == (iota((128, 128), 1) & 63), 0.25, 0.0)
    high = stack.astype(BF)
    rest = stack - high.astype(F32)
    middle = rest.astype(BF)
    low = (rest - middle.astype(F32)).astype(BF)
    parts = mm(jnp.concatenate([high, middle, low], axis=0), pool.astype(BF))
    pooled = parts[:80] + (parts[80:160] + parts[160:])
    for f in range(5):
        data = pooled[16 * f : 16 * f + 16] * keep[...]
        for q in range(16):
            send[q, f : f + 1, :] = data[q : q + 1]


def segment(recv, group, sections, low, high):
    left = iota((1, 128), 1) < 64
    first = None
    for j in range(GROUP):
        a, b, c, ra, rb = (
            jnp.where(left, recv[j, f : f + 1, :], recv[GROUP - 1 - j, f : f + 1, :]) for f in range(5)
        )
        section = GROUP * group + jnp.where(left, j, GROUP - 1 - j)
        ends = (section == 0) | (section == sections - 1)
        extra = jnp.where(ends, SPRING + ANCHOR, 2 * SPRING + ANCHOR)
        a, c = a + extra, c + extra
        if j == 0:
            d, y = (a, b, c), (ra, rb)
            eight, none = jnp.full((1, 128), SPRING), jnp.zeros((1, 128))
            cc = (eight, none, none, eight)
        else:
            inv = tuple(SPRING * x for x in inv_sym(*d))
            iy = mul21(full(inv), y)
            d = (a - SPRING * inv[0], b - SPRING * inv[1], c - SPRING * inv[2])
            y = (ra + iy[0], rb + iy[1])
            cc = mul22(full(inv), cc)
        rows = d + y + cc
        if j < 8:
            for f, x in enumerate(rows):
                low[f, j : j + 1, :] = x
            for f, x in enumerate((a, b, c, ra, rb)):
                low[9 + f, j : j + 1, :] = x
        else:
            for f, x in enumerate(rows):
                high[f, GROUP - 1 - j : GROUP - j, :] = x
    return rows


def link_step(front, back, pk, pv):
    d, y, c = front[:3], front[3:5], front[5:]
    bd, by, bc = back[:3], back[3:5], back[5:]
    ea, eb, ec, ed = (
        bd[0] - SPRING * pk[0],
        bd[1] - SPRING * pk[1],
        bd[1] - SPRING * pk[2],
        bd[2] - SPRING * pk[3],
    )
    r = 1.0 / (ea * ed - eb * ec)
    einv = (ed * r, -eb * r, -ec * r, ea * r)
    dinv = full(inv_sym(*d))
    through = mul22(c, pk)
    lead = mul22(through, einv)
    gain = mul22(lead, bc)
    gain = (gain[0] + SPRING, gain[1], gain[2], gain[3] + SPRING)
    load = mul21(lead, (by[0] + SPRING * pv[0], by[1] + SPRING * pv[1]))
    held = mul21(c, pv)
    return mul22(dinv, gain), mul21(dinv, (y[0] + held[0] + load[0], y[1] + held[1] + load[1]))


def links(recv, group, groups, own):
    left = iota((1, 128), 1) < 64
    none = jnp.zeros((1, 128))
    pk, pv = (none,) * 4, (none,) * 2
    limit = jnp.where(left, group, groups - 1 - group)
    for j in range(groups - 1):
        here = [recv[j, f : f + 1, :] for f in range(9)]
        there = [recv[groups - 1 - j, f : f + 1, :] for f in range(9)]
        front = tuple(jnp.where(left, x, z) for x, z in zip(here, there))
        back = tuple(half_turn(jnp.where(left, z, x)) for x, z in zip(here, there))
        nk, nv = link_step(front, back, pk, pv)
        use = limit > j
        pk = tuple(jnp.where(use, n, o) for n, o in zip(nk, pk))
        pv = tuple(jnp.where(use, n, o) for n, o in zip(nv, pv))
    nk, nv = link_step(own, tuple(half_turn(x) for x in own), pk, pv)
    rk, rv = tuple(half_turn(x) for x in pk), tuple(half_turn(x) for x in pv)
    t = mul22(nk, rk)
    a, b, c, d = 1.0 - t[0], -t[1], -t[2], 1.0 - t[3]
    r = 1.0 / (a * d - b * c)
    rhs = mul21(nk, rv)
    w = mul21((d * r, -b * r, -c * r, a * r), (rhs[0] + nv[0], rhs[1] + nv[1]))
    x = mul21(rk, w)
    return half_turn(x[0] + rv[0]), half_turn(x[1] + rv[1])


def interior(low, high, bound):
    lo = [low[f] for f in range(14)]
    hi = [high[f] for f in range(9)]
    other = [half_turn(x) for x in hi[:5]]
    d = [lo[f] + other[f] - lo[9 + f] for f in range(5)]
    near = mul21(lo[5:9], bound)
    far = mul21(hi[5:9], bound)
    rhs = [d[3 + n] + near[n] + half_turn(far[n]) for n in range(2)]
    return mul21(full(inv_sym(*d[:3])), rhs)


def kernel(
    sections,
    strips,
    image,
    w1_hbm,
    w2_hbm,
    marks_hbm,
    out_ref,
    w1_ref,
    w2_ref,
    marks_ref,
    keep,
    nwin,
    owin,
    sel,
    w1b,
    w2p,
    nxs,
    oxs,
    nfm,
    ofm,
    lall,
    rall,
    scores,
    mom,
    send_a,
    recv_a,
    low,
    high,
    send_b,
    recv_b,
    send_c,
    recv_c,
    local_sem,
    isend,
    irecv,
    asend,
    arecv,
    bsend,
    brecv,
    csend,
    crecv,
):
    s, r = lax.axis_index("gz"), lax.axis_index("gy")
    groups = sections // GROUP
    group, k = lax.div(s, GROUP), lax.rem(s, GROUP)
    after, before = lax.rem(s + 1, sections), lax.rem(s + sections - 1, sections)
    down, up = lax.rem(r + 1, strips), lax.rem(r + strips - 1, strips)
    mates = [GROUP * group + lax.rem(k + o, GROUP) for o in range(GROUP)]
    peers = [GROUP * lax.rem(group + o, groups) + k for o in range(groups)]

    local = pltpu.make_async_copy(image, owin.at[pl.ds(16, 128)], local_sem.at[0])
    smalls = [
        pltpu.make_async_copy(src, dst, local_sem.at[n + 1])
        for n, (src, dst) in enumerate(((w1_hbm, w1_ref), (w2_hbm, w2_ref), (marks_hbm, marks_ref)))
    ]
    for move in smalls:
        move.start()
    local.start()
    barrier = pltpu.get_barrier_semaphore()
    partners = [
        (before, r),
        (after, r),
        (before, up),
        (after, down),
        (before, down),
        (after, up),
        (s, down),
        (s, up),
    ]
    partners += [(m, r) for m in mates[1:]] + [(m, r) for m in peers[1:]]
    for place in partners:
        pl.semaphore_signal(barrier, inc=1, device_id=place, device_id_type=MESH)

    for move in smalls:
        move.wait()
    build_weights(w1_ref, w2_ref, sel, w1b, w2p)
    node_marks(marks_ref, s == sections - 1, keep)
    nxs[:, 0:16, :] = jnp.zeros((7, 16, 128), BF)
    oxs[:, 0:16, :] = jnp.zeros((7, 16, 128), BF)
    oxs[:, 160:176, :] = jnp.zeros((7, 16, 128), BF)

    pl.semaphore_wait(barrier, len(partners))

    def remote(src, dst, ssem, rsem, place):
        return pltpu.make_async_remote_copy(
            src_ref=src,
            dst_ref=dst,
            send_sem=ssem,
            recv_sem=rsem,
            device_id=place,
            device_id_type=MESH,
        )

    halo = remote(image.at[pl.ds(112, 16)], owin.at[pl.ds(0, 16)], isend.at[0], irecv.at[0], (s, down))
    def piece(row, target, n, place):
        return remote(
            image.at[pl.ds(row, 32)], nwin.at[pl.ds(target, 32)], isend.at[n], irecv.at[n], place
        )

    moves = [piece(96, 0, 1, (before, down))]
    moves += [piece(32 * c, 32 + 32 * c, 2 + c, (before, r)) for c in range(4)]
    moves += [piece(0, 160, 6, (before, up))]
    halo.start()
    for move in moves:
        move.start()
    local.wait()

    def loop(low, high, step):
        def run(i, carry):
            step(i)
            return carry

        lax.fori_loop(low, high, run, 0)

    split_columns(owin, 16, 128, sel, oxs)
    loop(2, 5, lambda i: conv_rows(oxs, w1b, ofm, 3, i))
    conv_rows(oxs, w1b, ofm, 1, 8)
    loop(3, 16, lambda i: own_pair(ofm, w2p, rall, i))
    halo.wait_recv()

    @pl.when(r == 0)
    def _():
        owin[0:16, :] = jnp.zeros((16, 512), BF)

    split_columns(owin, 0, 16, sel, oxs)
    conv_rows(oxs, w1b, ofm, 1, 0)
    for p in range(3):
        own_pair(ofm, w2p, rall, p)

    for half in range(2):
        for c in range(3):
            moves[3 * half + c].wait_recv()
        edge = 160 * half

        @pl.when(r == (strips - 1) * half)
        def _():
            nwin[edge : edge + 32, :] = jnp.zeros((32, 512), BF)

        split_columns(nwin, 96 * half, 96, sel, nxs)
        block = 6 * half
        conv_rows(nxs, w1b, nfm, 1, block)
        conv_rows(nxs, w1b, nfm, 1, block + 2)
        for g in (0,) if half == 0 else (5, 6):
            next_group(nfm, w2p, lall, 32 * r - 6, g)
        conv_rows(nxs, w1b, nfm, 1, block + 4)
        for g in range(1, 5) if half == 0 else range(7, 11):
            next_group(nfm, w2p, lall, 32 * r - 6, g)

    for p in range(AHEAD):
        score_pair(lall, rall, scores, p)
    for p in range(16):
        if p + AHEAD < 16:
            score_pair(lall, rall, scores, p + AHEAD)
        moments_pair(scores.at[p % BUFFERS], mom, p)

    node_blocks(mom, keep, send_a)
    moves_a = [
        remote(send_a.at[mates[o]  - GROUP * group], recv_a.at[k], asend.at[o - 1], arecv.at[o - 1], (mates[o], r))
        for o in far_first(GROUP)
    ]
    for move in moves_a:
        move.start()
    recv_a[k] = send_a[k]
    for move in moves_a:
        move.wait_recv()

    ends = segment(recv_a, group, sections, low, high)
    for f, x in enumerate(ends):
        send_b[f : f + 1, :] = x
    moves_b = [
        remote(send_b, recv_b.at[group], bsend.at[o - 1], brecv.at[o - 1], (peers[o], r))
        for o in far_first(groups)
    ]
    for move in moves_b:
        move.start()
    recv_b[group] = send_b[...]
    for move in moves_b:
        move.wait_recv()

    bound = links(recv_b, group, groups, ends)
    xa, xb = interior(low, high, bound)
    left8 = iota((8, 128), 1) < 64
    front = jnp.where(left8, xa, half_turn(xb))
    rear = jnp.where(left8, half_turn(xa), xb)
    for j in range(8):
        send_c[j] = front[j : j + 1]
        send_c[GROUP - 1 - j] = rear[j : j + 1]
    slot = 8 * lax.rem(k, 2) + lax.div(k, 2)
    moves_c = [
        remote(send_c.at[mates[o] - GROUP * group], recv_c.at[slot], csend.at[o - 1], crecv.at[o - 1], (mates[o], r))
        for o in far_first(GROUP)
    ]
    for move in moves_c:
        move.start()
    recv_c[slot] = send_c[k]
    for move in moves_c:
        move.wait_recv()
    even = jnp.concatenate([recv_c[q] for q in range(8)], axis=0)
    odd = jnp.concatenate([recv_c[q] for q in range(8, 16)], axis=0)
    out_ref[0] = jnp.where(left8, even, half_turn(odd))
    out_ref[1] = jnp.where(left8, half_turn(even), odd)
    for move in (halo, *moves, *moves_a, *moves_b, *moves_c):
        move.wait_send()


def body(sections, strips, image, conv_one, conv_two, tissue):
    groups = sections // GROUP
    vmem = pl.BlockSpec(memory_space=pltpu.VMEM)
    dma = pltpu.SemaphoreType.DMA
    out = pl.pallas_call(
        lambda *refs: kernel(sections, strips, *refs),
        out_shape=jax.ShapeDtypeStruct((2, 8, 128), F32),
        in_specs=[pl.BlockSpec(memory_space=pl.ANY)] * 4,
        out_specs=vmem,
        scratch_shapes=[
            pltpu.VMEM((16, 9), BF),
            pltpu.VMEM((32, 144), BF),
            pltpu.VMEM((8, 128), jnp.int32),
            pltpu.VMEM((16, 128), F32),
            pltpu.VMEM((192, 512), BF),
            pltpu.VMEM((144, 512), BF),
            pltpu.VMEM((256, 256), BF),
            pltpu.VMEM((384, 224), BF),
            pltpu.VMEM((32, 144), BF),
            pltpu.VMEM((7, 208, 128), BF),
            pltpu.VMEM((7, 176, 128), BF),
            pltpu.VMEM((12 * 384, 128), BF),
            pltpu.VMEM((10 * 384, 128), BF),
            pltpu.VMEM((44 * ROWS, 256), BF),
            pltpu.VMEM((16, 256, 256), BF),
            pltpu.VMEM((BUFFERS, 14 * ROWS, 256), F32),
            pltpu.VMEM((16, 8, 256), F32),
            pltpu.VMEM((GROUP, 5, 128), F32),
            pltpu.VMEM((GROUP, 5, 128), F32),
            pltpu.VMEM((14, 8, 128), F32),
            pltpu.VMEM((9, 8, 128), F32),
            pltpu.VMEM((9, 128), F32),
            pltpu.VMEM((groups, 9, 128), F32),
            pltpu.VMEM((GROUP, 1, 128), F32),
            pltpu.VMEM((GROUP, 1, 128), F32),
            dma((4,)),
            dma((7,)),
            dma((7,)),
            dma((GROUP - 1,)),
            dma((GROUP - 1,)),
            dma((groups - 1,)),
            dma((groups - 1,)),
            dma((GROUP - 1,)),
            dma((GROUP - 1,)),
        ],
        compiler_params=pltpu.CompilerParams(
            collective_id=0, has_side_effects=True, vmem_limit_bytes=VMEM_LIMIT
        ),
    )(image.reshape(128, 512), conv_one, conv_two, tissue.reshape(8, 128))
    return out.reshape(2, 1, 1024)


def solution(mesh):
    sections, strips = mesh.shape["gz"], mesh.shape["gy"]
    placed = (P("gz", "gy", None), P(), P(), P("gz", "gy"))
    return jax.shard_map(
        lambda *args: body(sections, strips, *args),
        mesh=mesh,
        in_specs=placed,
        out_specs=P(None, "gz", "gy"),
        check_vma=False,
    )
```

```python
import jax
import jax.numpy as jnp
from jax import lax
from jax.experimental import pallas as pl
from jax.experimental.pallas import tpu as pltpu
from jax.sharding import PartitionSpec as P

BF, F32 = jnp.bfloat16, jnp.float32
MESH = pl.DeviceIdType.MESH
GROUP = 16
SPRING, ANCHOR = 8.0, 0.02
AHEAD, BUFFERS = 2, 4
VMEM_LIMIT = 60 * 1024 * 1024
ROWS = 32
SCALE = 32 ** (-0.5) * 1.4426950408889634


def iota(shape, dim):
    return lax.broadcasted_iota(jnp.int32, shape, dim)


def mm(left, right):
    return jnp.dot(left, right, preferred_element_type=F32)


def far_first(count):
    return sorted(range(1, count), key=lambda o: -min(o, count - o))


def half_turn(x):
    return pltpu.roll(x, 64, 1)


def inv_sym(a, b, c):
    r = 1.0 / (a * c - b * b)
    return c * r, -b * r, a * r


def mul22(l, r):
    return (
        l[0] * r[0] + l[1] * r[2],
        l[0] * r[1] + l[1] * r[3],
        l[2] * r[0] + l[3] * r[2],
        l[2] * r[1] + l[3] * r[3],
    )


def mul21(l, v):
    return l[0] * v[0] + l[1] * v[1], l[2] * v[0] + l[3] * v[1]


def full(sym):
    return sym[0], sym[1], sym[1], sym[2]


def build_weights(w1_ref, w2_ref, sel, w1b, w2p):
    col = iota((256, 256), 1)
    sel[...] = jnp.where(iota((256, 256), 0) == 4 * (col & 63) + (col >> 6), 1.0, 0.0).astype(BF)
    tap, col = iota((9, 256), 0), iota((9, 256), 1)
    a = (tap * 11) >> 5
    da = (col & 31) - 15 - a
    db = (col >> 5) - (tap - 3 * a)
    w1 = w1_ref[...]
    base = jnp.concatenate(
        [mm(w1, jnp.where((da == 0) & (db == 2 * b), 1.0, 0.0).astype(BF)) for b in range(3)], axis=0
    )
    for f in range(8):
        moved = base if f == 0 else pltpu.roll(base, 2 * f, 1)
        w1b[48 * f : 48 * f + 48, :] = moved[:, :224].astype(BF)
    k, n = iota((144, 144), 0), iota((144, 144), 1)
    ab = n >> 4
    perm = jnp.where(k == 9 * (n & 15) + ab, 1.0, 0.0).astype(BF)
    w2p[...] = mm(w2_ref[...], perm).astype(BF)


def split_columns(window, low, rows, sel, xs):
    span = slice(16 + low, 16 + low + rows)
    out = [mm(window[low : low + rows, 256 * h : 256 * h + 256], sel[...]) for h in range(2)]
    lane = iota((rows, 128), 1)
    for n in range(2):
        one, two = (x[:, 128 * n : 128 * n + 128] for x in out)
        even = jnp.where(lane < 64, one, half_turn(two))
        odd = jnp.where(lane < 64, half_turn(one), two)
        for phase, x in ((2 * n, even), (2 * n + 1, odd)):
            xs[phase + 3, span, :] = x.astype(BF)
            if phase > 0:
                xs[phase - 1, span, :] = jnp.where(lane == 0, 0.0, pltpu.roll(x, 1, 1)).astype(BF)


def conv_rows(xs, w1b, fm, half, low):
    def column(block):
        start = 16 * block if isinstance(block, int) else pl.multiple_of(16 * block, 16)
        return jnp.concatenate([xs[v, pl.ds(start, 32), :] for v in range(7)], axis=0)

    right = jnp.concatenate([column(low), column(low + half)], axis=1)
    out = jnp.maximum(mm(w1b[...], right), 0.0).astype(BF)
    for n in range(2):
        start = 384 * (low + n * half)
        start = start if isinstance(low, int) else pl.multiple_of(start, 128)
        fm[pl.ds(start, 384), :] = out[:, 128 * n : 128 * n + 128]


def conv_features(fm, w2p, first, count):
    starts = [96 * (first + q) - 48 for q in range(count)]
    if not isinstance(first, int):
        starts = [pl.multiple_of(x, 16) for x in starts]
    right = jnp.concatenate([fm[pl.ds(x, 144), :] for x in starts], axis=1)
    return jnp.maximum(mm(w2p[...], right), 0.0).astype(BF).astype(F32)


def own_pair(fm, w2p, rall, p):
    feats = conv_features(fm, w2p, 4 + 2 * p, 2)
    chunk = (iota((32, 256), 1) & 127) >> 4
    rall[p] = jnp.concatenate(
        [jnp.where(chunk == m, feats, 0.0) for m in range(8)], axis=0
    ).astype(BF)


def next_group(fm, w2p, lall, row_base, g):
    feats = conv_features(fm, w2p, 4 * g + 2, 4)
    stack = jnp.concatenate(
        [
            feats[:, 128 * q : 128 * q + 128] * (row_base + 4 * g + q < 128).astype(F32)
            for q in range(4)
        ],
        axis=0,
    )
    stack = stack.astype(BF)
    place = jnp.where(iota((144, 128), 0) == iota((144, 128), 1) + 6, 1.0, 0.0).astype(BF)
    ext = lax.dot_general(place, stack, (((1,), (1,)), ((), ())), preferred_element_type=F32)
    ext = ext.astype(BF)
    rot = [ext] + [pltpu.roll(ext, 32 * k, 1) for k in range(1, 4)]
    lane = iota((32, 128), 1) >> 5
    for q in range(4):
        halves = []
        for h in range(2):
            pick = [rot[(g4 - q) % 4][64 * h + 16 * g4 : 64 * h + 16 * g4 + 32] for g4 in range(4)]
            halves.append(
                jnp.where(
                    lane < 2,
                    jnp.where(lane == 0, pick[0], pick[1]),
                    jnp.where(lane == 2, pick[2], pick[3]),
                )
            )
        lall[128 * g + 32 * q : 128 * g + 32 * q + 32, :] = jnp.concatenate(
            halves, axis=1
        )


def score_pair(lall, rall, scores, p):
    scores[p % BUFFERS] = mm(lall[64 * p : 64 * p + 14 * ROWS, :], rall[p])


def moments_pair(scores, mom, p):
    shift = iota((ROWS, 128), 0) - (iota((ROWS, 128), 1) & 15)
    valid = (shift >= 0) & (shift <= 12)
    b = (shift - 6).astype(F32)
    for par in range(2):
        cols = slice(128 * par, 128 * par + 128)

        def at(n):
            return scores[ROWS * (n + par) : ROWS * (n + par) + ROWS, cols]

        high = at(0)
        for n in range(1, 13):
            high = jnp.maximum(high, at(n))
        top = jnp.max(jnp.where(valid, high, -3e38), axis=0, keepdims=True)
        t0 = t1 = t2 = None
        for n in range(12, -1, -1):
            e = jnp.exp2((at(n) - top) * SCALE)
            t0 = e if t0 is None else t0 + e
            t1 = t0 if t1 is None else t1 + t0
            t2 = t1 if t2 is None else t2 + t1
        t0 = jnp.where(valid, t0, 0.0)
        t1 = jnp.where(valid, t1, 0.0)
        t2 = jnp.where(valid, t2, 0.0)
        tb = t0 * b
        for field, term in enumerate((t0, t1, t2, tb, tb * b, t1 * b)):
            mom[p, field : field + 1, cols] = jnp.sum(term, axis=0, keepdims=True)


def node_marks(marks_ref, last, keep):
    spread = jnp.where((iota((16, 8), 0) >> 1) == iota((16, 8), 1), 1.0, 0.0)
    marks = mm(spread, marks_ref[...].astype(F32))
    same = (iota((16, 128), 0) & 1) == (iota((16, 128), 1) >> 6)
    keep[...] = jnp.where(same, marks, half_turn(marks)) * jnp.where(last, 0.0, 1.0)


def node_blocks(mom, keep, send):
    m0, m1, m2, mb, mbb, mab = (mom[:, f, :] for f in range(6))
    r = 1.0 / m0
    n1, mean_b = m1 * r, mb * r
    mean_a = n1 - 7.0
    var_a = (2.0 * m2 - 15.0 * m1) * r + 49.0 - mean_a * mean_a + 1.0
    var_b = mbb * r - mean_b * mean_b + 1.0
    cov = mab * r - n1 * mean_b
    i_aa, i_ab, i_bb = inv_sym(var_a, cov, var_b)
    p_a = i_aa * mean_a + i_ab * mean_b
    p_b = i_ab * mean_a + i_bb * mean_b
    stack = jnp.concatenate([x[:, :128] + x[:, 128:] for x in (i_aa, i_ab, i_bb, p_a, p_b)], axis=0)
    pool = jnp.where((iota((128, 128), 0) >> 1) == (iota((128, 128), 1) & 63), 0.25, 0.0)
    high = stack.astype(BF)
    rest = stack - high.astype(F32)
    middle = rest.astype(BF)
    low = (rest - middle.astype(F32)).astype(BF)
    parts = mm(jnp.concatenate([high, middle, low], axis=0), pool.astype(BF))
    pooled = parts[:80] + (parts[80:160] + parts[160:])
    for f in range(5):
        data = pooled[16 * f : 16 * f + 16] * keep[...]
        for q in range(16):
            send[q, f : f + 1, :] = data[q : q + 1]


def segment(recv, group, sections, low, high):
    left = iota((1, 128), 1) < 64
    first = None
    for j in range(GROUP):
        a, b, c, ra, rb = (
            jnp.where(left, recv[j, f : f + 1, :], recv[GROUP - 1 - j, f : f + 1, :]) for f in range(5)
        )
        section = GROUP * group + jnp.where(left, j, GROUP - 1 - j)
        ends = (section == 0) | (section == sections - 1)
        extra = jnp.where(ends, SPRING + ANCHOR, 2 * SPRING + ANCHOR)
        a, c = a + extra, c + extra
        if j == 0:
            d, y = (a, b, c), (ra, rb)
            eight, none = jnp.full((1, 128), SPRING), jnp.zeros((1, 128))
            cc = (eight, none, none, eight)
        else:
            inv = tuple(SPRING * x for x in inv_sym(*d))
            iy = mul21(full(inv), y)
            d = (a - SPRING * inv[0], b - SPRING * inv[1], c - SPRING * inv[2])
            y = (ra + iy[0], rb + iy[1])
            cc = mul22(full(inv), cc)
        rows = d + y + cc
        if j < 8:
            for f, x in enumerate(rows):
                low[f, j : j + 1, :] = x
            for f, x in enumerate((a, b, c, ra, rb)):
                low[9 + f, j : j + 1, :] = x
        else:
            for f, x in enumerate(rows):
                high[f, GROUP - 1 - j : GROUP - j, :] = x
    return rows


def link_step(front, back, pk, pv):
    d, y, c = front[:3], front[3:5], front[5:]
    bd, by, bc = back[:3], back[3:5], back[5:]
    ea, eb, ec, ed = (
        bd[0] - SPRING * pk[0],
        bd[1] - SPRING * pk[1],
        bd[1] - SPRING * pk[2],
        bd[2] - SPRING * pk[3],
    )
    r = 1.0 / (ea * ed - eb * ec)
    einv = (ed * r, -eb * r, -ec * r, ea * r)
    dinv = full(inv_sym(*d))
    through = mul22(c, pk)
    lead = mul22(through, einv)
    gain = mul22(lead, bc)
    gain = (gain[0] + SPRING, gain[1], gain[2], gain[3] + SPRING)
    load = mul21(lead, (by[0] + SPRING * pv[0], by[1] + SPRING * pv[1]))
    held = mul21(c, pv)
    return mul22(dinv, gain), mul21(dinv, (y[0] + held[0] + load[0], y[1] + held[1] + load[1]))


def links(recv, group, groups, own):
    left = iota((1, 128), 1) < 64
    none = jnp.zeros((1, 128))
    pk, pv = (none,) * 4, (none,) * 2
    limit = jnp.where(left, group, groups - 1 - group)
    for j in range(groups - 1):
        here = [recv[j, f : f + 1, :] for f in range(9)]
        there = [recv[groups - 1 - j, f : f + 1, :] for f in range(9)]
        front = tuple(jnp.where(left, x, z) for x, z in zip(here, there))
        back = tuple(half_turn(jnp.where(left, z, x)) for x, z in zip(here, there))
        nk, nv = link_step(front, back, pk, pv)
        use = limit > j
        pk = tuple(jnp.where(use, n, o) for n, o in zip(nk, pk))
        pv = tuple(jnp.where(use, n, o) for n, o in zip(nv, pv))
    nk, nv = link_step(own, tuple(half_turn(x) for x in own), pk, pv)
    rk, rv = tuple(half_turn(x) for x in pk), tuple(half_turn(x) for x in pv)
    t = mul22(nk, rk)
    a, b, c, d = 1.0 - t[0], -t[1], -t[2], 1.0 - t[3]
    r = 1.0 / (a * d - b * c)
    rhs = mul21(nk, rv)
    w = mul21((d * r, -b * r, -c * r, a * r), (rhs[0] + nv[0], rhs[1] + nv[1]))
    x = mul21(rk, w)
    return half_turn(x[0] + rv[0]), half_turn(x[1] + rv[1])


def interior(low, high, bound):
    lo = [low[f] for f in range(14)]
    hi = [high[f] for f in range(9)]
    other = [half_turn(x) for x in hi[:5]]
    d = [lo[f] + other[f] - lo[9 + f] for f in range(5)]
    near = mul21(lo[5:9], bound)
    far = mul21(hi[5:9], bound)
    rhs = [d[3 + n] + near[n] + half_turn(far[n]) for n in range(2)]
    return mul21(full(inv_sym(*d[:3])), rhs)


def kernel(
    sections,
    strips,
    image,
    w1_hbm,
    w2_hbm,
    marks_hbm,
    out_ref,
    w1_ref,
    w2_ref,
    marks_ref,
    keep,
    nwin,
    owin,
    sel,
    w1b,
    w2p,
    nxs,
    oxs,
    nfm,
    ofm,
    lall,
    rall,
    scores,
    mom,
    send_a,
    recv_a,
    low,
    high,
    send_b,
    recv_b,
    send_c,
    recv_c,
    local_sem,
    isend,
    irecv,
    asend,
    arecv,
    bsend,
    brecv,
    csend,
    crecv,
):
    s, r = lax.axis_index("gz"), lax.axis_index("gy")
    groups = sections // GROUP
    group, k = lax.div(s, GROUP), lax.rem(s, GROUP)
    after, before = lax.rem(s + 1, sections), lax.rem(s + sections - 1, sections)
    down, up = lax.rem(r + 1, strips), lax.rem(r + strips - 1, strips)
    mates = [GROUP * group + lax.rem(k + o, GROUP) for o in range(GROUP)]
    peers = [GROUP * lax.rem(group + o, groups) + k for o in range(groups)]

    local = pltpu.make_async_copy(image, owin.at[pl.ds(16, 128)], local_sem.at[0])
    smalls = [
        pltpu.make_async_copy(src, dst, local_sem.at[n + 1])
        for n, (src, dst) in enumerate(((w1_hbm, w1_ref), (w2_hbm, w2_ref), (marks_hbm, marks_ref)))
    ]
    for move in smalls:
        move.start()
    local.start()
    barrier = pltpu.get_barrier_semaphore()
    partners = [
        (before, r),
        (after, r),
        (before, up),
        (after, down),
        (before, down),
        (after, up),
        (s, down),
        (s, up),
    ]
    partners += [(m, r) for m in mates[1:]] + [(m, r) for m in peers[1:]]
    for place in partners:
        pl.semaphore_signal(barrier, inc=1, device_id=place, device_id_type=MESH)

    for move in smalls:
        move.wait()
    build_weights(w1_ref, w2_ref, sel, w1b, w2p)
    node_marks(marks_ref, s == sections - 1, keep)
    nxs[:, 0:16, :] = jnp.zeros((7, 16, 128), BF)
    oxs[:, 0:32, :] = jnp.zeros((7, 32, 128), BF)

    pl.semaphore_wait(barrier, len(partners))

    def remote(src, dst, ssem, rsem, place):
        return pltpu.make_async_remote_copy(
            src_ref=src,
            dst_ref=dst,
            send_sem=ssem,
            recv_sem=rsem,
            device_id=place,
            device_id_type=MESH,
        )

    halo = remote(owin.at[pl.ds(128, 16)], owin.at[pl.ds(0, 16)], isend.at[0], irecv.at[0], (s, down))
    def piece(row, target, n, place):
        return remote(
            owin.at[pl.ds(16 + row, 32)], nwin.at[pl.ds(target, 32)], isend.at[n], irecv.at[n], place
        )

    moves = [piece(96, 0, 1, (before, down))]
    moves += [piece(32 * c, 32 + 32 * c, 2 + c, (before, r)) for c in range(4)]
    moves += [piece(0, 160, 6, (before, up))]
    local.wait()
    halo.start()
    for move in moves:
        move.start()

    def loop(low, high, step):
        def run(i, carry):
            step(i)
            return carry

        lax.fori_loop(low, high, run, 0)

    split_columns(owin, 16, 128, sel, oxs)
    loop(2, 5, lambda i: conv_rows(oxs, w1b, ofm, 3, i))
    conv_rows(oxs, w1b, ofm, 7, 1)
    loop(1, 16, lambda i: own_pair(ofm, w2p, rall, i))
    halo.wait_recv()

    @pl.when(r == 0)
    def _():
        owin[0:16, :] = jnp.zeros((16, 512), BF)

    split_columns(owin, 0, 16, sel, oxs)
    conv_rows(oxs, w1b, ofm, 1, 0)
    own_pair(ofm, w2p, rall, 0)

    done, group_done, queue, behind = 0, 0, [], []
    for first, last in ((0, 6),):
        for c in range(first, last):
            moves[c].wait_recv()
            if c in (0, 5):

                @pl.when(r == (0 if c == 0 else strips - 1))
                def _():
                    nwin[32 * c : 32 * c + 32, :] = jnp.zeros((32, 512), BF)

        split_columns(nwin, 32 * first, 32 * (last - first), sel, nxs)
        for g in range(group_done, 2 * last - 1):
            while done < min(last, (g + 1) // 2 + 1 + 1):
                conv_rows(nxs, w1b, nfm, 1, 2 * done)
                done += 1
            next_group(nfm, w2p, lall, 32 * r - 6, g)
            group_done = g + 1
            queue += [p for p in range(16) if (2 * p + 13) // 4 == g]
            while len(queue) > 2:
                p = queue.pop(0)
                score_pair(lall, rall, scores, p)
                behind.append(p)
                if len(behind) > AHEAD:
                    p = behind.pop(0)
                    moments_pair(scores.at[p % BUFFERS], mom, p)
    while behind or queue:
        if behind:
            p = behind.pop(0)
            moments_pair(scores.at[p % BUFFERS], mom, p)
        if queue:
            p = queue.pop(0)
            score_pair(lall, rall, scores, p)
            behind.append(p)

    node_blocks(mom, keep, send_a)
    moves_a = [
        remote(send_a.at[mates[o]  - GROUP * group], recv_a.at[k], asend.at[o - 1], arecv.at[o - 1], (mates[o], r))
        for o in far_first(GROUP)
    ]
    for move in moves_a:
        move.start()
    recv_a[k] = send_a[k]
    for move in moves_a:
        move.wait_recv()

    ends = segment(recv_a, group, sections, low, high)
    for f, x in enumerate(ends):
        send_b[f : f + 1, :] = x
    moves_b = [
        remote(send_b, recv_b.at[group], bsend.at[o - 1], brecv.at[o - 1], (peers[o], r))
        for o in far_first(groups)
    ]
    for move in moves_b:
        move.start()
    recv_b[group] = send_b[...]
    for move in moves_b:
        move.wait_recv()

    bound = links(recv_b, group, groups, ends)
    xa, xb = interior(low, high, bound)
    left8 = iota((8, 128), 1) < 64
    front = jnp.where(left8, xa, half_turn(xb))
    rear = jnp.where(left8, half_turn(xa), xb)
    for j in range(8):
        send_c[j] = front[j : j + 1]
        send_c[GROUP - 1 - j] = rear[j : j + 1]
    slot = 8 * lax.rem(k, 2) + lax.div(k, 2)
    moves_c = [
        remote(send_c.at[mates[o] - GROUP * group], recv_c.at[slot], csend.at[o - 1], crecv.at[o - 1], (mates[o], r))
        for o in far_first(GROUP)
    ]
    for move in moves_c:
        move.start()
    recv_c[slot] = send_c[k]
    for move in moves_c:
        move.wait_recv()
    even = jnp.concatenate([recv_c[q] for q in range(8)], axis=0)
    odd = jnp.concatenate([recv_c[q] for q in range(8, 16)], axis=0)
    out_ref[0] = jnp.where(left8, even, half_turn(odd))
    out_ref[1] = jnp.where(left8, half_turn(even), odd)
    for move in (halo, *moves, *moves_a, *moves_b, *moves_c):
        move.wait_send()


def body(sections, strips, image, conv_one, conv_two, tissue):
    groups = sections // GROUP
    vmem = pl.BlockSpec(memory_space=pltpu.VMEM)
    dma = pltpu.SemaphoreType.DMA
    out = pl.pallas_call(
        lambda *refs: kernel(sections, strips, *refs),
        out_shape=jax.ShapeDtypeStruct((2, 8, 128), F32),
        in_specs=[pl.BlockSpec(memory_space=pl.ANY)] * 4,
        out_specs=vmem,
        scratch_shapes=[
            pltpu.VMEM((16, 9), BF),
            pltpu.VMEM((32, 144), BF),
            pltpu.VMEM((8, 128), jnp.int32),
            pltpu.VMEM((16, 128), F32),
            pltpu.VMEM((192, 512), BF),
            pltpu.VMEM((144, 512), BF),
            pltpu.VMEM((256, 256), BF),
            pltpu.VMEM((384, 224), BF),
            pltpu.VMEM((32, 144), BF),
            pltpu.VMEM((7, 208, 128), BF),
            pltpu.VMEM((7, 176, 128), BF),
            pltpu.VMEM((12 * 384, 128), BF),
            pltpu.VMEM((10 * 384, 128), BF),
            pltpu.VMEM((44 * ROWS, 256), BF),
            pltpu.VMEM((16, 256, 256), BF),
            pltpu.VMEM((BUFFERS, 14 * ROWS, 256), F32),
            pltpu.VMEM((16, 8, 256), F32),
            pltpu.VMEM((GROUP, 5, 128), F32),
            pltpu.VMEM((GROUP, 5, 128), F32),
            pltpu.VMEM((14, 8, 128), F32),
            pltpu.VMEM((9, 8, 128), F32),
            pltpu.VMEM((9, 128), F32),
            pltpu.VMEM((groups, 9, 128), F32),
            pltpu.VMEM((GROUP, 1, 128), F32),
            pltpu.VMEM((GROUP, 1, 128), F32),
            dma((4,)),
            dma((7,)),
            dma((7,)),
            dma((GROUP - 1,)),
            dma((GROUP - 1,)),
            dma((groups - 1,)),
            dma((groups - 1,)),
            dma((GROUP - 1,)),
            dma((GROUP - 1,)),
        ],
        compiler_params=pltpu.CompilerParams(
            collective_id=0, has_side_effects=True, vmem_limit_bytes=VMEM_LIMIT
        ),
    )(image.reshape(128, 512), conv_one, conv_two, tissue.reshape(8, 128))
    return out.reshape(2, 1, 1024)


def solution(mesh):
    sections, strips = mesh.shape["gz"], mesh.shape["gy"]
    placed = (P("gz", "gy", None), P(), P(), P("gz", "gy"))
    return jax.shard_map(
        lambda *args: body(sections, strips, *args),
        mesh=mesh,
        in_specs=placed,
        out_specs=P(None, "gz", "gy"),
        check_vma=False,
    )
```

```python
import jax
import jax.numpy as jnp
from jax import lax
from jax.experimental import pallas as pl
from jax.experimental.pallas import tpu as pltpu
from jax.sharding import PartitionSpec as P

BF, F32 = jnp.bfloat16, jnp.float32
MESH = pl.DeviceIdType.MESH
GROUP = 16
SPRING, ANCHOR = 8.0, 0.02
AHEAD, BUFFERS = 2, 4
VMEM_LIMIT = 60 * 1024 * 1024
ROWS = 32
SCALE = 32 ** (-0.5) * 1.4426950408889634


def iota(shape, dim):
    return lax.broadcasted_iota(jnp.int32, shape, dim)


def mm(left, right):
    return jnp.dot(left, right, preferred_element_type=F32)


def far_first(count):
    return sorted(range(1, count), key=lambda o: -min(o, count - o))


def half_turn(x):
    return pltpu.roll(x, 64, 1)


def inv_sym(a, b, c):
    r = 1.0 / (a * c - b * b)
    return c * r, -b * r, a * r


def mul22(l, r):
    return (
        l[0] * r[0] + l[1] * r[2],
        l[0] * r[1] + l[1] * r[3],
        l[2] * r[0] + l[3] * r[2],
        l[2] * r[1] + l[3] * r[3],
    )


def mul21(l, v):
    return l[0] * v[0] + l[1] * v[1], l[2] * v[0] + l[3] * v[1]


def full(sym):
    return sym[0], sym[1], sym[1], sym[2]


def build_weights(w1_ref, w2_ref, sel, w1b, w2p):
    col = iota((256, 256), 1)
    sel[...] = jnp.where(iota((256, 256), 0) == 4 * (col & 63) + (col >> 6), 1.0, 0.0).astype(BF)
    tap, col = iota((9, 256), 0), iota((9, 256), 1)
    a = (tap * 11) >> 5
    da = (col & 31) - 15 - a
    db = (col >> 5) - (tap - 3 * a)
    w1 = w1_ref[...]
    base = jnp.concatenate(
        [mm(w1, jnp.where((da == 0) & (db == 2 * b), 1.0, 0.0).astype(BF)) for b in range(3)], axis=0
    )
    for f in range(8):
        moved = base if f == 0 else pltpu.roll(base, 2 * f, 1)
        w1b[48 * f : 48 * f + 48, :] = moved[:, :224].astype(BF)
    k, n = iota((144, 144), 0), iota((144, 144), 1)
    ab = n >> 4
    perm = jnp.where(k == 9 * (n & 15) + ab, 1.0, 0.0).astype(BF)
    w2p[...] = mm(w2_ref[...], perm).astype(BF)


def split_columns(window, low, rows, sel, xs):
    span = slice(16 + low, 16 + low + rows)
    out = [mm(window[low : low + rows, 256 * h : 256 * h + 256], sel[...]) for h in range(2)]
    lane = iota((rows, 128), 1)
    for n in range(2):
        one, two = (x[:, 128 * n : 128 * n + 128] for x in out)
        even = jnp.where(lane < 64, one, half_turn(two))
        odd = jnp.where(lane < 64, half_turn(one), two)
        for phase, x in ((2 * n, even), (2 * n + 1, odd)):
            xs[phase + 3, span, :] = x.astype(BF)
            if phase > 0:
                xs[phase - 1, span, :] = jnp.where(lane == 0, 0.0, pltpu.roll(x, 1, 1)).astype(BF)


def conv_rows(xs, w1b, fm, half, low):
    def column(block):
        start = 16 * block if isinstance(block, int) else pl.multiple_of(16 * block, 16)
        return jnp.concatenate([xs[v, pl.ds(start, 32), :] for v in range(7)], axis=0)

    right = jnp.concatenate([column(low), column(low + half)], axis=1)
    out = jnp.maximum(mm(w1b[...], right), 0.0).astype(BF)
    for n in range(2):
        start = 384 * (low + n * half)
        start = start if isinstance(low, int) else pl.multiple_of(start, 128)
        fm[pl.ds(start, 384), :] = out[:, 128 * n : 128 * n + 128]


def conv_features(fm, w2p, first, count):
    starts = [96 * (first + q) - 48 for q in range(count)]
    if not isinstance(first, int):
        starts = [pl.multiple_of(x, 16) for x in starts]
    right = jnp.concatenate([fm[pl.ds(x, 144), :] for x in starts], axis=1)
    return jnp.maximum(mm(w2p[...], right), 0.0).astype(BF).astype(F32)


def own_pair(fm, w2p, rall, p):
    feats = conv_features(fm, w2p, 4 + 2 * p, 2)
    chunk = (iota((32, 256), 1) & 127) >> 4
    rall[p] = jnp.concatenate(
        [jnp.where(chunk == m, feats, 0.0) for m in range(8)], axis=0
    ).astype(BF)


def next_group(fm, w2p, lall, row_base, g):
    feats = conv_features(fm, w2p, 4 * g + 2, 4)
    stack = jnp.concatenate(
        [
            feats[:, 128 * q : 128 * q + 128] * (row_base + 4 * g + q < 128).astype(F32)
            for q in range(4)
        ],
        axis=0,
    )
    stack = stack.astype(BF)
    place = jnp.where(iota((144, 128), 0) == iota((144, 128), 1) + 6, 1.0, 0.0).astype(BF)
    ext = lax.dot_general(place, stack, (((1,), (1,)), ((), ())), preferred_element_type=F32)
    ext = ext.astype(BF)
    rot = [ext] + [pltpu.roll(ext, 32 * k, 1) for k in range(1, 4)]
    lane = iota((32, 128), 1) >> 5
    for q in range(4):
        halves = []
        for h in range(2):
            pick = [rot[(g4 - q) % 4][64 * h + 16 * g4 : 64 * h + 16 * g4 + 32] for g4 in range(4)]
            halves.append(
                jnp.where(
                    lane < 2,
                    jnp.where(lane == 0, pick[0], pick[1]),
                    jnp.where(lane == 2, pick[2], pick[3]),
                )
            )
        lall[128 * g + 32 * q : 128 * g + 32 * q + 32, :] = jnp.concatenate(
            halves, axis=1
        )


def score_pair(lall, rall, scores, p):
    scores[p % BUFFERS] = mm(lall[64 * p : 64 * p + 14 * ROWS, :], rall[p])


def moments_pair(scores, mom, p):
    shift = iota((ROWS, 128), 0) - (iota((ROWS, 128), 1) & 15)
    valid = (shift >= 0) & (shift <= 12)
    b = (shift - 6).astype(F32)
    for par in range(2):
        cols = slice(128 * par, 128 * par + 128)

        def at(n):
            return scores[ROWS * (n + par) : ROWS * (n + par) + ROWS, cols]

        high = at(0)
        for n in range(1, 13):
            high = jnp.maximum(high, at(n))
        top = jnp.max(jnp.where(valid, high, -3e38), axis=0, keepdims=True)
        t0 = t1 = t2 = None
        for n in range(12, -1, -1):
            e = jnp.exp2((at(n) - top) * SCALE)
            t0 = e if t0 is None else t0 + e
            t1 = t0 if t1 is None else t1 + t0
            t2 = t1 if t2 is None else t2 + t1
        t0 = jnp.where(valid, t0, 0.0)
        t1 = jnp.where(valid, t1, 0.0)
        t2 = jnp.where(valid, t2, 0.0)
        tb = t0 * b
        for field, term in enumerate((t0, t1, t2, tb, tb * b, t1 * b)):
            mom[p, field : field + 1, cols] = jnp.sum(term, axis=0, keepdims=True)


def node_marks(marks_ref, last, keep):
    spread = jnp.where((iota((16, 8), 0) >> 1) == iota((16, 8), 1), 1.0, 0.0)
    marks = mm(spread, marks_ref[...].astype(F32))
    same = (iota((16, 128), 0) & 1) == (iota((16, 128), 1) >> 6)
    keep[...] = jnp.where(same, marks, half_turn(marks)) * jnp.where(last, 0.0, 1.0)


def node_blocks(mom, keep, send):
    m0, m1, m2, mb, mbb, mab = (mom[:, f, :] for f in range(6))
    r = 1.0 / m0
    n1, mean_b = m1 * r, mb * r
    mean_a = n1 - 7.0
    var_a = (2.0 * m2 - 15.0 * m1) * r + 49.0 - mean_a * mean_a + 1.0
    var_b = mbb * r - mean_b * mean_b + 1.0
    cov = mab * r - n1 * mean_b
    i_aa, i_ab, i_bb = inv_sym(var_a, cov, var_b)
    p_a = i_aa * mean_a + i_ab * mean_b
    p_b = i_ab * mean_a + i_bb * mean_b
    stack = jnp.concatenate([x[:, :128] + x[:, 128:] for x in (i_aa, i_ab, i_bb, p_a, p_b)], axis=0)
    pool = jnp.where((iota((128, 128), 0) >> 1) == (iota((128, 128), 1) & 63), 0.25, 0.0)
    high = stack.astype(BF)
    rest = stack - high.astype(F32)
    middle = rest.astype(BF)
    low = (rest - middle.astype(F32)).astype(BF)
    parts = mm(jnp.concatenate([high, middle, low], axis=0), pool.astype(BF))
    pooled = parts[:80] + (parts[80:160] + parts[160:])
    for f in range(5):
        send[:, f, :] = pooled[16 * f : 16 * f + 16] * keep[...]


def segment(recv, group, sections, low, high):
    left = iota((1, 128), 1) < 64
    first = None
    for j in range(GROUP):
        a, b, c, ra, rb = (
            jnp.where(left, recv[j, f : f + 1, :], recv[GROUP - 1 - j, f : f + 1, :]) for f in range(5)
        )
        section = GROUP * group + jnp.where(left, j, GROUP - 1 - j)
        ends = (section == 0) | (section == sections - 1)
        extra = jnp.where(ends, SPRING + ANCHOR, 2 * SPRING + ANCHOR)
        a, c = a + extra, c + extra
        if j == 0:
            d, y = (a, b, c), (ra, rb)
            eight, none = jnp.full((1, 128), SPRING), jnp.zeros((1, 128))
            cc = (eight, none, none, eight)
        else:
            inv = tuple(SPRING * x for x in inv_sym(*d))
            iy = mul21(full(inv), y)
            d = (a - SPRING * inv[0], b - SPRING * inv[1], c - SPRING * inv[2])
            y = (ra + iy[0], rb + iy[1])
            cc = mul22(full(inv), cc)
        rows = d + y + cc
        if j < 8:
            for f, x in enumerate(rows):
                low[f, j : j + 1, :] = x
            for f, x in enumerate((a, b, c, ra, rb)):
                low[9 + f, j : j + 1, :] = x
        else:
            for f, x in enumerate(rows):
                high[f, GROUP - 1 - j : GROUP - j, :] = x
    return rows


def link_step(front, back, pk, pv):
    d, y, c = front[:3], front[3:5], front[5:]
    bd, by, bc = back[:3], back[3:5], back[5:]
    ea, eb, ec, ed = (
        bd[0] - SPRING * pk[0],
        bd[1] - SPRING * pk[1],
        bd[1] - SPRING * pk[2],
        bd[2] - SPRING * pk[3],
    )
    r = 1.0 / (ea * ed - eb * ec)
    einv = (ed * r, -eb * r, -ec * r, ea * r)
    dinv = full(inv_sym(*d))
    through = mul22(c, pk)
    lead = mul22(through, einv)
    gain = mul22(lead, bc)
    gain = (gain[0] + SPRING, gain[1], gain[2], gain[3] + SPRING)
    load = mul21(lead, (by[0] + SPRING * pv[0], by[1] + SPRING * pv[1]))
    held = mul21(c, pv)
    return mul22(dinv, gain), mul21(dinv, (y[0] + held[0] + load[0], y[1] + held[1] + load[1]))


def links(recv, group, groups, own):
    left = iota((1, 128), 1) < 64
    none = jnp.zeros((1, 128))
    pk, pv = (none,) * 4, (none,) * 2
    limit = jnp.where(left, group, groups - 1 - group)
    for j in range(groups - 1):
        here = [recv[j, f : f + 1, :] for f in range(9)]
        there = [recv[groups - 1 - j, f : f + 1, :] for f in range(9)]
        front = tuple(jnp.where(left, x, z) for x, z in zip(here, there))
        back = tuple(half_turn(jnp.where(left, z, x)) for x, z in zip(here, there))
        nk, nv = link_step(front, back, pk, pv)
        use = limit > j
        pk = tuple(jnp.where(use, n, o) for n, o in zip(nk, pk))
        pv = tuple(jnp.where(use, n, o) for n, o in zip(nv, pv))
    nk, nv = link_step(own, tuple(half_turn(x) for x in own), pk, pv)
    rk, rv = tuple(half_turn(x) for x in pk), tuple(half_turn(x) for x in pv)
    t = mul22(nk, rk)
    a, b, c, d = 1.0 - t[0], -t[1], -t[2], 1.0 - t[3]
    r = 1.0 / (a * d - b * c)
    rhs = mul21(nk, rv)
    w = mul21((d * r, -b * r, -c * r, a * r), (rhs[0] + nv[0], rhs[1] + nv[1]))
    x = mul21(rk, w)
    return half_turn(x[0] + rv[0]), half_turn(x[1] + rv[1])


def interior(low, high, bound):
    lo = [low[f] for f in range(14)]
    hi = [high[f] for f in range(9)]
    other = [half_turn(x) for x in hi[:5]]
    d = [lo[f] + other[f] - lo[9 + f] for f in range(5)]
    near = mul21(lo[5:9], bound)
    far = mul21(hi[5:9], bound)
    rhs = [d[3 + n] + near[n] + half_turn(far[n]) for n in range(2)]
    return mul21(full(inv_sym(*d[:3])), rhs)


def kernel(
    sections,
    strips,
    image,
    w1_hbm,
    w2_hbm,
    marks_hbm,
    out_ref,
    w1_ref,
    w2_ref,
    marks_ref,
    keep,
    nwin,
    owin,
    sel,
    w1b,
    w2p,
    nxs,
    oxs,
    nfm,
    ofm,
    lall,
    rall,
    scores,
    mom,
    send_a,
    recv_a,
    low,
    high,
    send_b,
    recv_b,
    send_c,
    recv_c,
    local_sem,
    isend,
    irecv,
    asend,
    arecv,
    bsend,
    brecv,
    csend,
    crecv,
):
    s, r = lax.axis_index("gz"), lax.axis_index("gy")
    groups = sections // GROUP
    group, k = lax.div(s, GROUP), lax.rem(s, GROUP)
    after, before = lax.rem(s + 1, sections), lax.rem(s + sections - 1, sections)
    down, up = lax.rem(r + 1, strips), lax.rem(r + strips - 1, strips)
    mates = [GROUP * group + lax.rem(k + o, GROUP) for o in range(GROUP)]
    peers = [GROUP * lax.rem(group + o, groups) + k for o in range(groups)]

    local = pltpu.make_async_copy(image, owin.at[pl.ds(16, 128)], local_sem.at[0])
    smalls = [
        pltpu.make_async_copy(src, dst, local_sem.at[n + 1])
        for n, (src, dst) in enumerate(((w1_hbm, w1_ref), (w2_hbm, w2_ref), (marks_hbm, marks_ref)))
    ]
    for move in smalls:
        move.start()
    local.start()
    barrier = pltpu.get_barrier_semaphore()
    partners = [
        (before, r),
        (after, r),
        (before, up),
        (after, down),
        (before, down),
        (after, up),
        (s, down),
        (s, up),
    ]
    partners += [(m, r) for m in mates[1:]] + [(m, r) for m in peers[1:]]
    for place in partners:
        pl.semaphore_signal(barrier, inc=1, device_id=place, device_id_type=MESH)

    for move in smalls:
        move.wait()
    build_weights(w1_ref, w2_ref, sel, w1b, w2p)
    node_marks(marks_ref, s == sections - 1, keep)
    nxs[:, 0:16, :] = jnp.zeros((7, 16, 128), BF)
    oxs[:, 0:32, :] = jnp.zeros((7, 32, 128), BF)

    pl.semaphore_wait(barrier, len(partners))

    def remote(src, dst, ssem, rsem, place):
        return pltpu.make_async_remote_copy(
            src_ref=src,
            dst_ref=dst,
            send_sem=ssem,
            recv_sem=rsem,
            device_id=place,
            device_id_type=MESH,
        )

    halo = remote(owin.at[pl.ds(128, 16)], owin.at[pl.ds(0, 16)], isend.at[0], irecv.at[0], (s, down))
    def piece(row, target, n, place):
        return remote(
            owin.at[pl.ds(16 + row, 32)], nwin.at[pl.ds(target, 32)], isend.at[n], irecv.at[n], place
        )

    moves = [piece(96, 0, 1, (before, down))]
    moves += [piece(32 * c, 32 + 32 * c, 2 + c, (before, r)) for c in range(4)]
    moves += [piece(0, 160, 6, (before, up))]
    local.wait()
    halo.start()
    for move in moves:
        move.start()

    def loop(low, high, step):
        def run(i, carry):
            step(i)
            return carry

        lax.fori_loop(low, high, run, 0)

    split_columns(owin, 16, 128, sel, oxs)
    loop(2, 5, lambda i: conv_rows(oxs, w1b, ofm, 3, i))
    conv_rows(oxs, w1b, ofm, 7, 1)
    loop(1, 16, lambda i: own_pair(ofm, w2p, rall, i))
    halo.wait_recv()

    @pl.when(r == 0)
    def _():
        owin[0:16, :] = jnp.zeros((16, 512), BF)

    split_columns(owin, 0, 16, sel, oxs)
    conv_rows(oxs, w1b, ofm, 1, 0)
    own_pair(ofm, w2p, rall, 0)

    done, group_done, queue, behind = 0, 0, [], []
    for first, last in ((0, 6),):
        for c in range(first, last):
            moves[c].wait_recv()
            if c in (0, 5):

                @pl.when(r == (0 if c == 0 else strips - 1))
                def _():
                    nwin[32 * c : 32 * c + 32, :] = jnp.zeros((32, 512), BF)

        split_columns(nwin, 32 * first, 32 * (last - first), sel, nxs)
        for g in range(group_done, 2 * last - 1):
            while done < min(last, (g + 1) // 2 + 1 + 1):
                conv_rows(nxs, w1b, nfm, 1, 2 * done)
                done += 1
            next_group(nfm, w2p, lall, 32 * r - 6, g)
            group_done = g + 1
            queue += [p for p in range(16) if (2 * p + 13) // 4 == g]
            while len(queue) > 4:
                p = queue.pop(0)
                score_pair(lall, rall, scores, p)
                behind.append(p)
                if len(behind) > AHEAD:
                    p = behind.pop(0)
                    moments_pair(scores.at[p % BUFFERS], mom, p)
    while behind or queue:
        if behind:
            p = behind.pop(0)
            moments_pair(scores.at[p % BUFFERS], mom, p)
        if queue:
            p = queue.pop(0)
            score_pair(lall, rall, scores, p)
            behind.append(p)

    node_blocks(mom, keep, send_a)
    moves_a = [
        remote(send_a.at[mates[o]  - GROUP * group], recv_a.at[k], asend.at[o - 1], arecv.at[o - 1], (mates[o], r))
        for o in far_first(GROUP)
    ]
    for move in moves_a:
        move.start()
    recv_a[k] = send_a[k]
    for move in (halo, *moves):
        move.wait_send()
    for move in moves_a:
        move.wait_recv()

    ends = segment(recv_a, group, sections, low, high)
    for f, x in enumerate(ends):
        send_b[f : f + 1, :] = x
    moves_b = [
        remote(send_b, recv_b.at[group], bsend.at[o - 1], brecv.at[o - 1], (peers[o], r))
        for o in far_first(groups)
    ]
    for move in moves_b:
        move.start()
    recv_b[group] = send_b[...]
    for move in moves_a:
        move.wait_send()
    for move in moves_b:
        move.wait_recv()

    bound = links(recv_b, group, groups, ends)
    xa, xb = interior(low, high, bound)
    left8 = iota((8, 128), 1) < 64
    front = jnp.where(left8, xa, half_turn(xb))
    rear = jnp.where(left8, half_turn(xa), xb)
    send_c[0:8, 0, :] = front
    send_c[8:16, 0, :] = rear

    def place_of(m):
        return m + lax.div(m, 8) * (23 - 2 * m)

    slot = 8 * lax.rem(k, 2) + lax.div(k, 2)
    moves_c = [
        remote(send_c.at[place_of(mates[o] - GROUP * group)], recv_c.at[slot], csend.at[o - 1], crecv.at[o - 1], (mates[o], r))
        for o in far_first(GROUP)
    ]
    for move in moves_c:
        move.start()
    recv_c[slot] = send_c[place_of(k)]
    for move in moves_b + moves_c:
        move.wait_send()
    for move in moves_c:
        move.wait_recv()
    even = recv_c[0:8, 0, :]
    odd = recv_c[8:16, 0, :]
    out_ref[0] = jnp.where(left8, even, half_turn(odd))
    out_ref[1] = jnp.where(left8, half_turn(even), odd)


def body(sections, strips, image, conv_one, conv_two, tissue):
    groups = sections // GROUP
    vmem = pl.BlockSpec(memory_space=pltpu.VMEM)
    dma = pltpu.SemaphoreType.DMA
    out = pl.pallas_call(
        lambda *refs: kernel(sections, strips, *refs),
        out_shape=jax.ShapeDtypeStruct((2, 8, 128), F32),
        in_specs=[pl.BlockSpec(memory_space=pl.ANY)] * 4,
        out_specs=vmem,
        scratch_shapes=[
            pltpu.VMEM((16, 9), BF),
            pltpu.VMEM((32, 144), BF),
            pltpu.VMEM((8, 128), jnp.int32),
            pltpu.VMEM((16, 128), F32),
            pltpu.VMEM((192, 512), BF),
            pltpu.VMEM((144, 512), BF),
            pltpu.VMEM((256, 256), BF),
            pltpu.VMEM((384, 224), BF),
            pltpu.VMEM((32, 144), BF),
            pltpu.VMEM((7, 208, 128), BF),
            pltpu.VMEM((7, 176, 128), BF),
            pltpu.VMEM((12 * 384, 128), BF),
            pltpu.VMEM((10 * 384, 128), BF),
            pltpu.VMEM((44 * ROWS, 256), BF),
            pltpu.VMEM((16, 256, 256), BF),
            pltpu.VMEM((BUFFERS, 14 * ROWS, 256), F32),
            pltpu.VMEM((16, 8, 256), F32),
            pltpu.VMEM((GROUP, 5, 128), F32),
            pltpu.VMEM((GROUP, 5, 128), F32),
            pltpu.VMEM((14, 8, 128), F32),
            pltpu.VMEM((9, 8, 128), F32),
            pltpu.VMEM((9, 128), F32),
            pltpu.VMEM((groups, 9, 128), F32),
            pltpu.VMEM((GROUP, 1, 128), F32),
            pltpu.VMEM((GROUP, 1, 128), F32),
            dma((4,)),
            dma((7,)),
            dma((7,)),
            dma((GROUP - 1,)),
            dma((GROUP - 1,)),
            dma((groups - 1,)),
            dma((groups - 1,)),
            dma((GROUP - 1,)),
            dma((GROUP - 1,)),
        ],
        compiler_params=pltpu.CompilerParams(
            collective_id=0, has_side_effects=True, vmem_limit_bytes=VMEM_LIMIT
        ),
    )(image.reshape(128, 512), conv_one, conv_two, tissue.reshape(8, 128))
    return out.reshape(2, 1, 1024)


def solution(mesh):
    sections, strips = mesh.shape["gz"], mesh.shape["gy"]
    placed = (P("gz", "gy", None), P(), P(), P("gz", "gy"))
    return jax.shard_map(
        lambda *args: body(sections, strips, *args),
        mesh=mesh,
        in_specs=placed,
        out_specs=P(None, "gz", "gy"),
        check_vma=False,
    )
```

```python
import jax
import jax.numpy as jnp
from jax import lax
from jax.experimental import pallas as pl
from jax.experimental.pallas import tpu as pltpu
from jax.sharding import PartitionSpec as P

BF, F32 = jnp.bfloat16, jnp.float32
MESH = pl.DeviceIdType.MESH
GROUP = 16
SPRING, ANCHOR = 8.0, 0.02
AHEAD, BUFFERS = 2, 4
VMEM_LIMIT = 60 * 1024 * 1024
ROWS = 32
SCALE = 32 ** (-0.5) * 1.4426950408889634


def iota(shape, dim):
    return lax.broadcasted_iota(jnp.int32, shape, dim)


def mm(left, right):
    return jnp.dot(left, right, preferred_element_type=F32)


def far_first(count):
    return sorted(range(1, count), key=lambda o: -min(o, count - o))


def half_turn(x):
    return pltpu.roll(x, 64, 1)


def inv_sym(a, b, c):
    r = 1.0 / (a * c - b * b)
    return c * r, -b * r, a * r


def mul22(l, r):
    return (
        l[0] * r[0] + l[1] * r[2],
        l[0] * r[1] + l[1] * r[3],
        l[2] * r[0] + l[3] * r[2],
        l[2] * r[1] + l[3] * r[3],
    )


def mul21(l, v):
    return l[0] * v[0] + l[1] * v[1], l[2] * v[0] + l[3] * v[1]


def full(sym):
    return sym[0], sym[1], sym[1], sym[2]


def build_weights(w1_ref, w2_ref, sel, w1b, w2p):
    col = iota((256, 256), 1)
    sel[...] = jnp.where(iota((256, 256), 0) == 4 * (col & 63) + (col >> 6), 1.0, 0.0).astype(BF)
    tap, col = iota((9, 256), 0), iota((9, 256), 1)
    a = (tap * 11) >> 5
    da = (col & 31) - 15 - a
    db = (col >> 5) - (tap - 3 * a)
    w1 = w1_ref[...]
    base = jnp.concatenate(
        [mm(w1, jnp.where((da == 0) & (db == 2 * b), 1.0, 0.0).astype(BF)) for b in range(3)], axis=0
    )
    for f in range(8):
        moved = base if f == 0 else pltpu.roll(base, 2 * f, 1)
        w1b[48 * f : 48 * f + 48, :] = moved[:, :224].astype(BF)
    k, n = iota((144, 144), 0), iota((144, 144), 1)
    ab = n >> 4
    perm = jnp.where(k == 9 * (n & 15) + ab, 1.0, 0.0).astype(BF)
    w2p[...] = mm(w2_ref[...], perm).astype(BF)


def split_columns(window, low, rows, sel, xs):
    span = slice(16 + low, 16 + low + rows)
    out = [mm(window[low : low + rows, 256 * h : 256 * h + 256], sel[...]) for h in range(2)]
    lane = iota((rows, 128), 1)
    for n in range(2):
        one, two = (x[:, 128 * n : 128 * n + 128] for x in out)
        even = jnp.where(lane < 64, one, half_turn(two))
        odd = jnp.where(lane < 64, half_turn(one), two)
        for phase, x in ((2 * n, even), (2 * n + 1, odd)):
            xs[phase + 3, span, :] = x.astype(BF)
            if phase > 0:
                xs[phase - 1, span, :] = jnp.where(lane == 0, 0.0, pltpu.roll(x, 1, 1)).astype(BF)


def conv_rows(xs, w1b, fm, half, low):
    def column(block):
        start = 16 * block if isinstance(block, int) else pl.multiple_of(16 * block, 16)
        return jnp.concatenate([xs[v, pl.ds(start, 32), :] for v in range(7)], axis=0)

    right = jnp.concatenate([column(low), column(low + half)], axis=1)
    out = jnp.maximum(mm(w1b[...], right), 0.0).astype(BF)
    for n in range(2):
        start = 384 * (low + n * half)
        start = start if isinstance(low, int) else pl.multiple_of(start, 128)
        fm[pl.ds(start, 384), :] = out[:, 128 * n : 128 * n + 128]


def conv_features(fm, w2p, first, count):
    starts = [96 * (first + q) - 48 for q in range(count)]
    if not isinstance(first, int):
        starts = [pl.multiple_of(x, 16) for x in starts]
    right = jnp.concatenate([fm[pl.ds(x, 144), :] for x in starts], axis=1)
    return jnp.maximum(mm(w2p[...], right), 0.0).astype(BF).astype(F32)


def own_pair(fm, w2p, rall, p):
    feats = conv_features(fm, w2p, 4 + 2 * p, 2)
    chunk = (iota((32, 256), 1) & 127) >> 4
    rall[p] = jnp.concatenate(
        [jnp.where(chunk == m, feats, 0.0) for m in range(8)], axis=0
    ).astype(BF)


def next_group(fm, w2p, lall, row_base, g):
    feats = conv_features(fm, w2p, 4 * g + 2, 4)
    stack = jnp.concatenate(
        [
            feats[:, 128 * q : 128 * q + 128] * (row_base + 4 * g + q < 128).astype(F32)
            for q in range(4)
        ],
        axis=0,
    )
    stack = stack.astype(BF)
    place = jnp.where(iota((144, 128), 0) == iota((144, 128), 1) + 6, 1.0, 0.0).astype(BF)
    ext = lax.dot_general(place, stack, (((1,), (1,)), ((), ())), preferred_element_type=F32)
    ext = ext.astype(BF)
    rot = [ext] + [pltpu.roll(ext, 32 * k, 1) for k in range(1, 4)]
    lane = iota((32, 128), 1) >> 5
    for q in range(4):
        halves = []
        for h in range(2):
            pick = [rot[(g4 - q) % 4][64 * h + 16 * g4 : 64 * h + 16 * g4 + 32] for g4 in range(4)]
            halves.append(
                jnp.where(
                    lane < 2,
                    jnp.where(lane == 0, pick[0], pick[1]),
                    jnp.where(lane == 2, pick[2], pick[3]),
                )
            )
        lall[128 * g + 32 * q : 128 * g + 32 * q + 32, :] = jnp.concatenate(
            halves, axis=1
        )


def score_pair(lall, rall, scores, p):
    scores[p % BUFFERS] = mm(lall[64 * p : 64 * p + 14 * ROWS, :], rall[p])


def moments_pair(scores, mom, p):
    shift = iota((ROWS, 128), 0) - (iota((ROWS, 128), 1) & 15)
    valid = (shift >= 0) & (shift <= 12)
    b = (shift - 6).astype(F32)
    for par in range(2):
        cols = slice(128 * par, 128 * par + 128)

        def at(n):
            return scores[ROWS * (n + par) : ROWS * (n + par) + ROWS, cols]

        high = at(0)
        for n in range(1, 13):
            high = jnp.maximum(high, at(n))
        top = jnp.max(jnp.where(valid, high, -3e38), axis=0, keepdims=True)
        t0 = t1 = t2 = None
        for n in range(12, -1, -1):
            e = jnp.exp2((at(n) - top) * SCALE)
            t0 = e if t0 is None else t0 + e
            t1 = t0 if t1 is None else t1 + t0
            t2 = t1 if t2 is None else t2 + t1
        t0 = jnp.where(valid, t0, 0.0)
        t1 = jnp.where(valid, t1, 0.0)
        t2 = jnp.where(valid, t2, 0.0)
        tb = t0 * b
        for field, term in enumerate((t0, t1, t2, tb, tb * b, t1 * b)):
            mom[p, field : field + 1, cols] = jnp.sum(term, axis=0, keepdims=True)


def node_marks(marks_ref, last, keep):
    spread = jnp.where((iota((16, 8), 0) >> 1) == iota((16, 8), 1), 1.0, 0.0)
    marks = mm(spread, marks_ref[...].astype(F32))
    same = (iota((16, 128), 0) & 1) == (iota((16, 128), 1) >> 6)
    keep[...] = jnp.where(same, marks, half_turn(marks)) * jnp.where(last, 0.0, 1.0)


def node_blocks(mom, keep, send):
    m0, m1, m2, mb, mbb, mab = (mom[:, f, :] for f in range(6))
    r = 1.0 / m0
    n1, mean_b = m1 * r, mb * r
    mean_a = n1 - 7.0
    var_a = (2.0 * m2 - 15.0 * m1) * r + 49.0 - mean_a * mean_a + 1.0
    var_b = mbb * r - mean_b * mean_b + 1.0
    cov = mab * r - n1 * mean_b
    i_aa, i_ab, i_bb = inv_sym(var_a, cov, var_b)
    p_a = i_aa * mean_a + i_ab * mean_b
    p_b = i_ab * mean_a + i_bb * mean_b
    stack = jnp.concatenate([x[:, :128] + x[:, 128:] for x in (i_aa, i_ab, i_bb, p_a, p_b)], axis=0)
    pool = jnp.where((iota((128, 128), 0) >> 1) == (iota((128, 128), 1) & 63), 0.25, 0.0)
    high = stack.astype(BF)
    rest = stack - high.astype(F32)
    middle = rest.astype(BF)
    low = (rest - middle.astype(F32)).astype(BF)
    parts = mm(jnp.concatenate([high, middle, low], axis=0), pool.astype(BF))
    pooled = parts[:80] + (parts[80:160] + parts[160:])
    for f in range(5):
        send[:, f, :] = pooled[16 * f : 16 * f + 16] * keep[...]


def segment(recv, group, sections, low, high):
    left = iota((1, 128), 1) < 64
    first = None
    for j in range(GROUP):
        a, b, c, ra, rb = (
            jnp.where(left, recv[j, f : f + 1, :], recv[GROUP - 1 - j, f : f + 1, :]) for f in range(5)
        )
        section = GROUP * group + jnp.where(left, j, GROUP - 1 - j)
        ends = (section == 0) | (section == sections - 1)
        extra = jnp.where(ends, SPRING + ANCHOR, 2 * SPRING + ANCHOR)
        a, c = a + extra, c + extra
        if j == 0:
            d, y = (a, b, c), (ra, rb)
            eight, none = jnp.full((1, 128), SPRING), jnp.zeros((1, 128))
            cc = (eight, none, none, eight)
        else:
            inv = tuple(SPRING * x for x in inv_sym(*d))
            iy = mul21(full(inv), y)
            d = (a - SPRING * inv[0], b - SPRING * inv[1], c - SPRING * inv[2])
            y = (ra + iy[0], rb + iy[1])
            cc = mul22(full(inv), cc)
        rows = d + y + cc
        if j < 8:
            for f, x in enumerate(rows):
                low[f, j : j + 1, :] = x
            for f, x in enumerate((a, b, c, ra, rb)):
                low[9 + f, j : j + 1, :] = x
        else:
            for f, x in enumerate(rows):
                high[f, GROUP - 1 - j : GROUP - j, :] = x
    return rows


def link_step(front, back, pk, pv):
    d, y, c = front[:3], front[3:5], front[5:]
    bd, by, bc = back[:3], back[3:5], back[5:]
    ea, eb, ec, ed = (
        bd[0] - SPRING * pk[0],
        bd[1] - SPRING * pk[1],
        bd[1] - SPRING * pk[2],
        bd[2] - SPRING * pk[3],
    )
    r = 1.0 / (ea * ed - eb * ec)
    einv = (ed * r, -eb * r, -ec * r, ea * r)
    dinv = full(inv_sym(*d))
    through = mul22(c, pk)
    lead = mul22(through, einv)
    gain = mul22(lead, bc)
    gain = (gain[0] + SPRING, gain[1], gain[2], gain[3] + SPRING)
    load = mul21(lead, (by[0] + SPRING * pv[0], by[1] + SPRING * pv[1]))
    held = mul21(c, pv)
    return mul22(dinv, gain), mul21(dinv, (y[0] + held[0] + load[0], y[1] + held[1] + load[1]))


def links(recv, group, groups, own):
    left = iota((1, 128), 1) < 64
    none = jnp.zeros((1, 128))
    pk, pv = (none,) * 4, (none,) * 2
    limit = jnp.where(left, group, groups - 1 - group)
    for j in range(groups - 1):
        here = [recv[j, f : f + 1, :] for f in range(9)]
        there = [recv[groups - 1 - j, f : f + 1, :] for f in range(9)]
        front = tuple(jnp.where(left, x, z) for x, z in zip(here, there))
        back = tuple(half_turn(jnp.where(left, z, x)) for x, z in zip(here, there))
        nk, nv = link_step(front, back, pk, pv)
        use = limit > j
        pk = tuple(jnp.where(use, n, o) for n, o in zip(nk, pk))
        pv = tuple(jnp.where(use, n, o) for n, o in zip(nv, pv))
    nk, nv = link_step(own, tuple(half_turn(x) for x in own), pk, pv)
    rk, rv = tuple(half_turn(x) for x in pk), tuple(half_turn(x) for x in pv)
    t = mul22(nk, rk)
    a, b, c, d = 1.0 - t[0], -t[1], -t[2], 1.0 - t[3]
    r = 1.0 / (a * d - b * c)
    rhs = mul21(nk, rv)
    w = mul21((d * r, -b * r, -c * r, a * r), (rhs[0] + nv[0], rhs[1] + nv[1]))
    x = mul21(rk, w)
    return half_turn(x[0] + rv[0]), half_turn(x[1] + rv[1])


def interior(low, high, bound):
    lo = [low[f] for f in range(14)]
    hi = [high[f] for f in range(9)]
    other = [half_turn(x) for x in hi[:5]]
    d = [lo[f] + other[f] - lo[9 + f] for f in range(5)]
    near = mul21(lo[5:9], bound)
    far = mul21(hi[5:9], bound)
    rhs = [d[3 + n] + near[n] + half_turn(far[n]) for n in range(2)]
    return mul21(full(inv_sym(*d[:3])), rhs)


def kernel(
    sections,
    strips,
    image,
    w1_hbm,
    w2_hbm,
    marks_hbm,
    out_ref,
    w1_ref,
    w2_ref,
    marks_ref,
    keep,
    nwin,
    owin,
    sel,
    w1b,
    w2p,
    nxs,
    oxs,
    nfm,
    ofm,
    lall,
    rall,
    scores,
    mom,
    send_a,
    recv_a,
    low,
    high,
    send_b,
    recv_b,
    send_c,
    recv_c,
    local_sem,
    isend,
    irecv,
    asend,
    arecv,
    bsend,
    brecv,
    csend,
    crecv,
):
    s, r = lax.axis_index("gz"), lax.axis_index("gy")
    groups = sections // GROUP
    group, k = lax.div(s, GROUP), lax.rem(s, GROUP)
    after, before = lax.rem(s + 1, sections), lax.rem(s + sections - 1, sections)
    down, up = lax.rem(r + 1, strips), lax.rem(r + strips - 1, strips)
    mates = [GROUP * group + lax.rem(k + o, GROUP) for o in range(GROUP)]
    peers = [GROUP * lax.rem(group + o, groups) + k for o in range(groups)]

    local = pltpu.make_async_copy(image, owin.at[pl.ds(16, 128)], local_sem.at[0])
    smalls = [
        pltpu.make_async_copy(src, dst, local_sem.at[n + 1])
        for n, (src, dst) in enumerate(((w1_hbm, w1_ref), (w2_hbm, w2_ref), (marks_hbm, marks_ref)))
    ]
    for move in smalls:
        move.start()
    local.start()
    barrier = pltpu.get_barrier_semaphore()
    partners = [
        (before, r),
        (after, r),
        (before, up),
        (after, down),
        (before, down),
        (after, up),
        (s, down),
        (s, up),
    ]
    partners += [(m, r) for m in mates[1:]] + [(m, r) for m in peers[1:]]
    for place in partners:
        pl.semaphore_signal(barrier, inc=1, device_id=place, device_id_type=MESH)

    for move in smalls:
        move.wait()
    build_weights(w1_ref, w2_ref, sel, w1b, w2p)
    node_marks(marks_ref, s == sections - 1, keep)
    nxs[:, 0:16, :] = jnp.zeros((7, 16, 128), BF)
    oxs[:, 0:32, :] = jnp.zeros((7, 32, 128), BF)

    pl.semaphore_wait(barrier, len(partners))

    def remote(src, dst, ssem, rsem, place):
        return pltpu.make_async_remote_copy(
            src_ref=src,
            dst_ref=dst,
            send_sem=ssem,
            recv_sem=rsem,
            device_id=place,
            device_id_type=MESH,
        )

    halo = remote(owin.at[pl.ds(128, 16)], owin.at[pl.ds(0, 16)], isend.at[0], irecv.at[0], (s, down))
    def piece(row, target, n, place):
        return remote(
            owin.at[pl.ds(16 + row, 32)], nwin.at[pl.ds(target, 32)], isend.at[n], irecv.at[n], place
        )

    moves = [piece(96, 0, 1, (before, down))]
    moves += [piece(32 * c, 32 + 32 * c, 2 + c, (before, r)) for c in range(4)]
    moves += [piece(0, 160, 6, (before, up))]
    local.wait()
    halo.start()
    for move in moves:
        move.start()

    def loop(low, high, step):
        def run(i, carry):
            step(i)
            return carry

        lax.fori_loop(low, high, run, 0)

    split_columns(owin, 16, 128, sel, oxs)
    loop(2, 5, lambda i: conv_rows(oxs, w1b, ofm, 3, i))
    conv_rows(oxs, w1b, ofm, 7, 1)
    loop(1, 16, lambda i: own_pair(ofm, w2p, rall, i))
    halo.wait_recv()

    @pl.when(r == 0)
    def _():
        owin[0:16, :] = jnp.zeros((16, 512), BF)

    split_columns(owin, 0, 16, sel, oxs)
    conv_rows(oxs, w1b, ofm, 1, 0)
    own_pair(ofm, w2p, rall, 0)

    done, group_done, queue, behind = 0, 0, [], []
    for first, last in ((0, 6),):
        for c in range(first, last):
            moves[c].wait_recv()
            if c in (0, 5):

                @pl.when(r == (0 if c == 0 else strips - 1))
                def _():
                    nwin[32 * c : 32 * c + 32, :] = jnp.zeros((32, 512), BF)

        split_columns(nwin, 32 * first, 32 * (last - first), sel, nxs)
        for g in range(group_done, 2 * last - 1):
            while done < min(last, (g + 1) // 2 + 1 + 2):
                conv_rows(nxs, w1b, nfm, 1, 2 * done)
                done += 1
            next_group(nfm, w2p, lall, 32 * r - 6, g)
            group_done = g + 1
            queue += [p for p in range(16) if (2 * p + 13) // 4 == g]
            while len(queue) > 4:
                p = queue.pop(0)
                score_pair(lall, rall, scores, p)
                behind.append(p)
                if len(behind) > AHEAD:
                    p = behind.pop(0)
                    moments_pair(scores.at[p % BUFFERS], mom, p)
    while behind or queue:
        if behind:
            p = behind.pop(0)
            moments_pair(scores.at[p % BUFFERS], mom, p)
        if queue:
            p = queue.pop(0)
            score_pair(lall, rall, scores, p)
            behind.append(p)

    node_blocks(mom, keep, send_a)
    moves_a = [
        remote(send_a.at[mates[o]  - GROUP * group], recv_a.at[k], asend.at[o - 1], arecv.at[o - 1], (mates[o], r))
        for o in far_first(GROUP)
    ]
    for move in moves_a:
        move.start()
    recv_a[k] = send_a[k]
    for move in (halo, *moves):
        move.wait_send()
    for move in moves_a:
        move.wait_recv()

    ends = segment(recv_a, group, sections, low, high)
    for f, x in enumerate(ends):
        send_b[f : f + 1, :] = x
    moves_b = [
        remote(send_b, recv_b.at[group], bsend.at[o - 1], brecv.at[o - 1], (peers[o], r))
        for o in far_first(groups)
    ]
    for move in moves_b:
        move.start()
    recv_b[group] = send_b[...]
    for move in moves_a:
        move.wait_send()
    for move in moves_b:
        move.wait_recv()

    bound = links(recv_b, group, groups, ends)
    xa, xb = interior(low, high, bound)
    left8 = iota((8, 128), 1) < 64
    front = jnp.where(left8, xa, half_turn(xb))
    rear = jnp.where(left8, half_turn(xa), xb)
    send_c[0:8, 0, :] = front
    send_c[8:16, 0, :] = rear

    def place_of(m):
        return m + lax.div(m, 8) * (23 - 2 * m)

    slot = 8 * lax.rem(k, 2) + lax.div(k, 2)
    moves_c = [
        remote(send_c.at[place_of(mates[o] - GROUP * group)], recv_c.at[slot], csend.at[o - 1], crecv.at[o - 1], (mates[o], r))
        for o in far_first(GROUP)
    ]
    for move in moves_c:
        move.start()
    recv_c[slot] = send_c[place_of(k)]
    for move in moves_b + moves_c:
        move.wait_send()
    for move in moves_c:
        move.wait_recv()
    even = recv_c[0:8, 0, :]
    odd = recv_c[8:16, 0, :]
    out_ref[0] = jnp.where(left8, even, half_turn(odd))
    out_ref[1] = jnp.where(left8, half_turn(even), odd)


def body(sections, strips, image, conv_one, conv_two, tissue):
    groups = sections // GROUP
    vmem = pl.BlockSpec(memory_space=pltpu.VMEM)
    dma = pltpu.SemaphoreType.DMA
    out = pl.pallas_call(
        lambda *refs: kernel(sections, strips, *refs),
        out_shape=jax.ShapeDtypeStruct((2, 8, 128), F32),
        in_specs=[pl.BlockSpec(memory_space=pl.ANY)] * 4,
        out_specs=vmem,
        scratch_shapes=[
            pltpu.VMEM((16, 9), BF),
            pltpu.VMEM((32, 144), BF),
            pltpu.VMEM((8, 128), jnp.int32),
            pltpu.VMEM((16, 128), F32),
            pltpu.VMEM((192, 512), BF),
            pltpu.VMEM((144, 512), BF),
            pltpu.VMEM((256, 256), BF),
            pltpu.VMEM((384, 224), BF),
            pltpu.VMEM((32, 144), BF),
            pltpu.VMEM((7, 208, 128), BF),
            pltpu.VMEM((7, 176, 128), BF),
            pltpu.VMEM((12 * 384, 128), BF),
            pltpu.VMEM((10 * 384, 128), BF),
            pltpu.VMEM((44 * ROWS, 256), BF),
            pltpu.VMEM((16, 256, 256), BF),
            pltpu.VMEM((BUFFERS, 14 * ROWS, 256), F32),
            pltpu.VMEM((16, 8, 256), F32),
            pltpu.VMEM((GROUP, 5, 128), F32),
            pltpu.VMEM((GROUP, 5, 128), F32),
            pltpu.VMEM((14, 8, 128), F32),
            pltpu.VMEM((9, 8, 128), F32),
            pltpu.VMEM((9, 128), F32),
            pltpu.VMEM((groups, 9, 128), F32),
            pltpu.VMEM((GROUP, 1, 128), F32),
            pltpu.VMEM((GROUP, 1, 128), F32),
            dma((4,)),
            dma((7,)),
            dma((7,)),
            dma((GROUP - 1,)),
            dma((GROUP - 1,)),
            dma((groups - 1,)),
            dma((groups - 1,)),
            dma((GROUP - 1,)),
            dma((GROUP - 1,)),
        ],
        compiler_params=pltpu.CompilerParams(
            collective_id=0, has_side_effects=True, vmem_limit_bytes=VMEM_LIMIT
        ),
    )(image.reshape(128, 512), conv_one, conv_two, tissue.reshape(8, 128))
    return out.reshape(2, 1, 1024)


def solution(mesh):
    sections, strips = mesh.shape["gz"], mesh.shape["gy"]
    placed = (P("gz", "gy", None), P(), P(), P("gz", "gy"))
    return jax.shard_map(
        lambda *args: body(sections, strips, *args),
        mesh=mesh,
        in_specs=placed,
        out_specs=P(None, "gz", "gy"),
        check_vma=False,
    )
```
